512 devices in a mesh: shot: 2 (over core), tx: 8 (over z_hi, y), ty: 32 (over z_lo, x).
Axes of the slice: x: 4, y: 4, z: 16 (z_hi: 2, z_lo: 8; z = z_hi * 8 + z_lo), core: 2. Of those that a mesh axis runs over, the one named last changes fastest.
Arguments:
- forward_fields: float32 [2, 9, 128, 512, 128], P('shot', None, 'tx', 'ty'), may hold values from -6 to 6
- adjoint_fields: float32 [2, 9, 128, 512, 128], P('shot', None, 'tx', 'ty'), may hold values from -6 to 6
- lame_lambda: float32 [128, 512, 128], P('tx', 'ty'), may hold values from 1 to 4
- shear_modulus: float32 [128, 512, 128], P('tx', 'ty'), may hold values from 0.5 to 2
- density: float32 [128, 512, 128], P('tx', 'ty'), may hold values from 1 to 3
- source_cell: int32 [2], P('shot'), may hold values from 0 to 8388607
- source_amp: float32 [2], P('shot'), may hold values from 4 to 12
- receiver_cell: int32 [2, 256], P('shot'), may hold values from 0 to 8388607
- residual_amp: float32 [2, 256], P('shot'), may hold values from -16 to 16
Outputs:
- forward_next: float32 [2, 9, 128, 512, 128], P('shot', None, 'tx', 'ty')
- adjoint_next: float32 [2, 9, 128, 512, 128], P('shot', None, 'tx', 'ty')
- gradient: float32 [3, 128, 512, 128], P(None, 'tx', 'ty')
The draws below stay inside these ranges and needn't reach their ends.
Inputs may be any that keep to these rules, and one draw needn't show every extreme that they name: `source_cell`: each value is a flat index x * 512 * 128 + y * 128 + z of a grid cell. `receiver_cell`: each value is a flat index x * 512 * 128 + y * 128 + z of a grid cell; receivers may share cells.
All inputs are finite; a program needn't handle non-finite values.
Results may differ from the reference program's by a relative error of at most 0.0001.
Values sent between devices are 32-bit elements; how exact they have to be, the bound alone decides.
A program may use at most 64 MiB of HBM per device.

```python
import jax
import jax.numpy as jnp
from jax import lax

NZ = 128
REC = 256
NX = 128
NY = 512
SHOTS = 2


def touch_ends(values, own_key, least, high):
    dims = values.shape
    spot = [jax.random.randint(jax.random.fold_in(own_key, axis), (), 0, dims[axis]) for axis in range(len(dims))]
    values = values.at[tuple(spot)].set(least)
    longest = dims.index(max(dims))
    spot[longest] = (spot[longest] + 1) % dims[longest]
    return values.at[tuple(spot)].set(high)


def steps_of(stream_key, extent, pieces, smallest, top_value):
    loudness, own = 1.0, jax.random.fold_in(stream_key, 6)
    for axis_at, blocks in pieces:
        draws = jnp.exp(jax.random.uniform(jax.random.fold_in(own, axis_at), (blocks,), jnp.float32, smallest / len(pieces), top_value / len(pieces)))
        loudness = loudness * jnp.repeat(draws, extent[axis_at] // blocks).reshape([-1 if axis == axis_at else 1 for axis in range(len(extent))])
    return loudness


def gaussian(key, extent, deviation, most, cuts=(), held_as=jnp.bfloat16):
    gain = steps_of(key, extent, cuts, -0.22, 0.18) if cuts else 1.0
    array = jax.random.normal(key, extent, jnp.float32) * deviation * gain
    return jnp.minimum(jnp.maximum(array, -most), most).astype(held_as)


def setup_inputs(seed: int = 0) -> dict:
    splits = jax.random.split(jax.random.key(seed), 10)
    return {
        "forward_fields": gaussian(splits[0], (SHOTS, 9, NX, NY, NZ), 1.0, 6.0, ((0, 2), (2, 8), (3, 32)), jnp.float32),
        "adjoint_fields": gaussian(splits[1], (SHOTS, 9, NX, NY, NZ), 1.0, 6.0, ((0, 2), (2, 8), (3, 32)), jnp.float32),
        "lame_lambda": jnp.clip(1.0 + 3.0 * jax.random.uniform(splits[2], (NX, NY, NZ), jnp.float32) ** steps_of(splits[2], (NX, NY, NZ), ((0, 8), (1, 32)), -0.2, 0.2), 1.0, 4.0),
        "shear_modulus": jnp.clip(0.5 + 1.5 * jax.random.uniform(splits[3], (NX, NY, NZ), jnp.float32) ** steps_of(splits[3], (NX, NY, NZ), ((0, 8), (1, 32)), -0.2, 0.2), 0.5, 2.0),
        "density": jnp.clip(1.0 + 2.0 * jax.random.uniform(splits[4], (NX, NY, NZ), jnp.float32) ** steps_of(splits[4], (NX, NY, NZ), ((0, 8), (1, 32)), -0.2, 0.2), 1.0, 3.0),
        "source_cell": jax.random.randint(splits[5], (SHOTS,), 0, NX * NY * NZ).astype(jnp.int32),
        "source_amp": jnp.clip(4.0 + 8.0 * jax.random.uniform(splits[6], (SHOTS,), jnp.float32) ** steps_of(splits[6], (SHOTS,), ((0, 2),), -0.2, 0.2), 4.0, 12.0),
        "receiver_cell": touch_ends(jax.random.randint(splits[7], (SHOTS, REC), 0, NX * NY * NZ), jax.random.fold_in(splits[7], 1), 0, (NX * NY * NZ) - 1).astype(jnp.int32),
        "residual_amp": gaussian(splits[8], (SHOTS, REC), 4.0, 16.0, ((0, 2),), jnp.float32),
    }


near_coef = 9.0 / 8.0
far_coef = -1.0 / 24.0
time_step = 0.15


def shifted(padded, margin, rim_width, direction, offset):
    rank_count = padded.ndim
    sliced = padded
    for which in range(3):
        length = padded.shape[rank_count - 3 + which] - 2 * margin[which] + 2 * rim_width[which]
        begin_at = margin[which] - rim_width[which] + (offset if which == direction else 0)
        sliced = lax.slice_in_dim(sliced, begin_at, begin_at + length, axis=rank_count - 3 + which)
    return sliced


def derive(padded, margin, rim_width, direction, upward):
    if upward:
        return near_coef * (shifted(padded, margin, rim_width, direction, 1) - shifted(padded, margin, rim_width, direction, 0)) + far_coef * (shifted(padded, margin, rim_width, direction, 2) - shifted(padded, margin, rim_width, direction, -1))
    return near_coef * (shifted(padded, margin, rim_width, direction, 0) - shifted(padded, margin, rim_width, direction, -1)) + far_coef * (shifted(padded, margin, rim_width, direction, 1) - shifted(padded, margin, rim_width, direction, -2))


def accelerate(stress_ext, buoyancy, margin, rim_width):
    comps = [stress_ext[..., which, :, :, :] for which in range(6)]
    accel_x = derive(comps[0], margin, rim_width, 0, True) + derive(comps[3], margin, rim_width, 1, False) + derive(comps[4], margin, rim_width, 2, False)
    accel_y = derive(comps[3], margin, rim_width, 0, False) + derive(comps[1], margin, rim_width, 1, True) + derive(comps[5], margin, rim_width, 2, False)
    accel_z = derive(comps[4], margin, rim_width, 0, False) + derive(comps[5], margin, rim_width, 1, False) + derive(comps[2], margin, rim_width, 2, True)
    return jnp.stack([accel_x, accel_y, accel_z], axis=-4) * buoyancy


def strain_rates(velocity_ext, margin):
    flat_rim = (0, 0, 0)
    comps = [velocity_ext[..., which, :, :, :] for which in range(3)]
    return jnp.stack([
        derive(comps[0], margin, flat_rim, 0, False),
        derive(comps[1], margin, flat_rim, 1, False),
        derive(comps[2], margin, flat_rim, 2, False),
        derive(comps[0], margin, flat_rim, 1, True) + derive(comps[1], margin, flat_rim, 0, True),
        derive(comps[0], margin, flat_rim, 2, True) + derive(comps[2], margin, flat_rim, 0, True),
        derive(comps[1], margin, flat_rim, 2, True) + derive(comps[2], margin, flat_rim, 1, True),
    ], axis=-4)


def new_stress(stress_now, strain, lame_lambda, shear_modulus):
    trace = strain[..., 0, :, :, :] + strain[..., 1, :, :, :] + strain[..., 2, :, :, :]
    normal = stress_now[..., :3, :, :, :] + time_step * (lame_lambda * trace[..., None, :, :, :] + 2.0 * shear_modulus * strain[..., :3, :, :, :])
    shear = stress_now[..., 3:, :, :, :] + time_step * shear_modulus * strain[..., 3:, :, :, :]
    return jnp.concatenate([normal, shear], axis=-4)


def image_terms(strain_fwd, stress_adj, accel_fwd, velocity_adj):
    trace_fwd = strain_fwd[..., 0, :, :, :] + strain_fwd[..., 1, :, :, :] + strain_fwd[..., 2, :, :, :]
    trace_adj = stress_adj[..., 0, :, :, :] + stress_adj[..., 1, :, :, :] + stress_adj[..., 2, :, :, :]
    grad_lambda = -time_step * trace_fwd * trace_adj
    grad_shear = -time_step * jnp.sum(strain_fwd * stress_adj, axis=-4)
    grad_density = -time_step * jnp.sum(accel_fwd * velocity_adj, axis=-4)
    return jnp.stack([grad_lambda, grad_shear, grad_density], axis=-4)


def pad_cells(values):
    return jnp.pad(values, [(0, 0)] * (values.ndim - 3) + [(2, 2), (2, 2), (2, 2)])


def reference(forward_fields, adjoint_fields, lame_lambda, shear_modulus, density, source_cell, source_amp, receiver_cell, residual_amp):
    buoyancy = 1.0 / density
    cell_count = NX * NY * NZ
    margin = (2, 2, 2)

    def one_shot(summed, inputs):
        forward, adjoint, source, amount, receivers, values = inputs
        forward = forward.reshape(9, cell_count).at[3:6, source].add(amount).reshape(9, NX, NY, NZ)
        adjoint = adjoint.reshape(9, cell_count).at[3:6, receivers].add(values[None, :]).reshape(9, NX, NY, NZ)
        wavefields = jnp.stack([forward, adjoint])
        acceleration = accelerate(pad_cells(wavefields[:, 3:]), buoyancy, margin, (0, 0, 0))
        velocity = wavefields[:, :3] + time_step * acceleration
        strain = strain_rates(pad_cells(velocity), margin)
        stress = new_stress(wavefields[:, 3:], strain, lame_lambda, shear_modulus)
        summed = summed + image_terms(strain[0], stress[1], acceleration[0], velocity[1])
        stepped = jnp.concatenate([velocity, stress], axis=1)
        return summed, (stepped[0], stepped[1])

    start = jnp.zeros((3, NX, NY, NZ), jnp.float32)
    summed, outputs = lax.scan(one_shot, start, (forward_fields, adjoint_fields, source_cell, source_amp, receiver_cell, residual_amp))
    return outputs[0], outputs[1], summed
```

```python
import functools

import jax
import jax.numpy as jnp
from jax import lax
from jax.experimental import pallas as pl
from jax.experimental.pallas import tpu as pltpu
from jax.sharding import PartitionSpec as P

C1 = 9.0 / 8.0
C2 = -1.0 / 24.0
DT = 0.15
MESH = pl.DeviceIdType.MESH
F32 = jnp.float32
CHUNK = 4
XX, YY, ZZ, XY, XZ, YZ = range(6)


def step_kernel(
    fwd, adj, lam_h, mu_h, den_h, scell_h, samp_h, rcell_h, ramp_h,
    f_out, a_out, g_out,
    ST, VE, VO, AC, BU, LM, MU, ADD, rcell, ramp, scell, samp,
    ysend, yrecv, bysend, byrecv, y2sb, y2sa, y2rb, y2ra,
    xs_send, xv_send, xs_recv, xv_recv, rel, GL, GR,
    in_sem, y_ss, y_rs, x_ss, x_rs, rel_ss, rel_rs, g_ss, g_rs,
):
    s, tx, ty = lax.axis_index("shot"), lax.axis_index("tx"), lax.axis_index("ty")
    last = lax.axis_size("ty") - 1
    partner = (1 - s, tx, ty)

    has_l, has_r = tx > 0, tx < 7
    near_l, near_r = (tx > 0) & (tx != 4), (tx < 7) & (tx != 3)
    lower, upper = ty > 0, ty < last
    is3, is4 = tx == 3, tx == 4
    low_relay, high_relay = tx < 3, tx > 4

    bar = pltpu.get_barrier_semaphore()

    def greet(cond, dev):
        @pl.when(cond)
        def _():
            pl.semaphore_signal(bar, inc=1, device_id=dev, device_id_type=MESH)

    for j in range(3):
        greet(is3, (s, 5 + j, ty))
        greet(is4, (s, j, ty))
    greet(lower, (s, tx, ty - 1))
    greet(upper, (s, tx, ty + 1))
    greet(near_l, (s, tx - 1, ty))
    greet(near_r, (s, tx + 1, ty))
    greet(tx < 2, (s, 3, ty))
    greet(tx > 5, (s, 4, ty))
    pl.semaphore_signal(bar, inc=1, device_id=partner, device_id_type=MESH)

    loads = [
        (fwd.at[0, pl.ds(3, 6)], ST.at[0, :, pl.ds(2, 16), pl.ds(8, 16)]),
        (adj.at[0, pl.ds(3, 6)], ST.at[1, :, pl.ds(2, 16), pl.ds(8, 16)]),
        (rcell_h, rcell),
        (ramp_h, ramp),
        (scell_h, scell),
        (samp_h, samp),
        (den_h, BU.at[pl.ds(2, 16), pl.ds(8, 16)]),
        (fwd.at[0, pl.ds(0, 3)], VO.at[0]),
        (adj.at[0, pl.ds(0, 3)], VO.at[1]),
        (lam_h, LM),
        (mu_h, MU),
    ]
    copies = [pltpu.make_async_copy(a, b, in_sem.at[i]) for i, (a, b) in enumerate(loads)]
    for c in copies:
        c.start()

    def clear(cond, ref, idx):
        @pl.when(cond)
        def _():
            ref[idx] = jnp.zeros(ref.at[idx].shape, F32)

    for w in range(2):
        for c in (XX, XY, XZ):
            for lo in (0, 18):
                ST[w, c, lo:lo + 2, 8:24, :] = jnp.zeros((2, 16, 128), F32)
    for side, gone in ((0, ty == 0), (1, ty == last)):
        clear(gone, yrecv, side)
        clear(gone, byrecv, side)
    clear(ty == 0, y2rb, slice(None))
    clear(ty == last, y2ra, slice(None))
    for side, gone in ((0, tx == 0), (1, tx == 7)):
        clear(gone, xs_recv, side)
        clear(gone, xv_recv, side)
    xs_send[1, 10:12] = jnp.zeros((2, 16, 128), F32)
    xv_send[0, 8:10] = jnp.zeros((2, 16, 128), F32)
    for side in range(2):
        for w in range(2):
            xv_send[side, 10 + w] = jnp.zeros((16, 128), F32)
    ysend[0, :, 8:16, :] = jnp.zeros((16, 8, 128), F32)
    y2sa[:, 8:16, :] = jnp.zeros((16, 8, 128), F32)

    for c in copies[2:6]:
        c.wait()

    def place(cell):
        lx = (cell >> 16) - tx * 16
        ly = ((cell >> 7) & 511) - ty * 16
        inside = (lx >= 0) & (lx < 16) & (ly >= 0) & (ly < 16)
        return jnp.where(inside, lx * 16 + ly, -1), cell & 127

    column, depth = place(rcell[...])
    hot = (lax.broadcasted_iota(jnp.int32, (256, 256), 0) == column).astype(jnp.bfloat16)
    amount = jnp.where(lax.broadcasted_iota(jnp.int32, (128, 256), 0) == depth, ramp[...], 0.0)
    high = amount.astype(jnp.bfloat16)
    rest = amount - high.astype(F32)
    mid = rest.astype(jnp.bfloat16)
    low = (rest - mid.astype(F32)).astype(jnp.bfloat16)
    nt = (((1,), (1,)), ((), ()))
    added = sum(
        lax.dot_general(hot, part, nt, preferred_element_type=F32) for part in (low, mid, high)
    )
    ADD[...] = added.reshape(16, 16, 128)
    scol, sdep = place(scell[0])
    ssum = samp[0]
    copies[0].wait()
    copies[1].wait()

    def inject_rows(i, carry):
        shape = (2, 16, 128)
        col = (lax.broadcasted_iota(jnp.int32, shape, 0) + 2 * i) * 16 + lax.broadcasted_iota(jnp.int32, shape, 1)
        dep = lax.broadcasted_iota(jnp.int32, shape, 2)
        hit = (col == scol) & (dep == sdep)
        src = jnp.where(hit, ssum, 0.0)
        rows = pl.ds(2 + 2 * i, 2)
        for c in range(3):
            ST[0, c, rows, 8:24, :] = ST[0, c, rows, 8:24, :] + src
            ST[1, c, rows, 8:24, :] = ST[1, c, rows, 8:24, :] + ADD[pl.ds(2 * i, 2)]
        return carry

    lax.fori_loop(0, 8, inject_rows, 0)
    copies[6].wait()
    BU[2:18, 8:24, :] = DT / BU[2:18, 8:24, :]

    for w in range(2):
        layers = [(XX, 15), (XY, 14), (XY, 15), (XZ, 14), (XZ, 15)]
        for i, (c, x) in enumerate(layers):
            xs_send[0, 5 * w + i] = ST[w, c, 2 + x, 8:24, :]
        layers = [(XX, 0), (XX, 1), (XY, 0), (XZ, 0)]
        for i, (c, x) in enumerate(layers):
            xs_send[1, 4 * w + i] = ST[w, c, 2 + x, 8:24, :]
    for i in range(2):
        xs_send[0, 10 + i] = BU[16 + i, 8:24, :]
        xs_send[1, 8 + i] = BU[2 + i, 8:24, :]
    for w in range(2):
        rows = [(XY, 14, 2), (YZ, 14, 2), (YY, 15, 1), (XX, 15, 1), (XZ, 15, 1)]
        k = 7 * w
        for c, y, n in rows:
            ysend[0, :, k:k + n, :] = ST[w, c, 2:18, 8 + y:8 + y + n, :]
            k += n
        rows = [(XY, 0, 1), (YZ, 0, 1), (YY, 0, 2), (XX, 0, 2), (XZ, 0, 2)]
        k = 8 * w
        for c, y, n in rows:
            ysend[1, :, k:k + n, :] = ST[w, c, 2:18, 8 + y:8 + y + n, :]
            k += n
    for e, x in ((0, 0), (1, 14)):
        bysend[0, e] = BU[2 + x:4 + x, 16:24, :]
        bysend[1, e] = BU[2 + x:4 + x, 8:16, :]

    def one(cond):
        return jnp.where(cond, 1, 0)

    peers = 2 + one(lower) + one(upper) + one(near_l) + one(near_r) + one(is3 | is4)
    pl.semaphore_wait(bar, peers)

    def remote(src, dst, ss, rs, dev):
        return pltpu.make_async_remote_copy(
            src_ref=src, dst_ref=dst, send_sem=ss, recv_sem=rs, device_id=dev, device_id_type=MESH
        )

    def x_copy(side, kind, j):
        src = (xs_send, xv_send)[kind].at[side, pl.ds(CHUNK * j, CHUNK)]
        dst = (xs_recv, xv_recv)[kind].at[side, pl.ds(CHUNK * j, CHUNK)]
        dev = (s, tx + 1 if side == 0 else tx - 1, ty)
        return remote(src, dst, x_ss.at[side, kind, j], x_rs.at[side, kind, j], dev)

    def to_relay(side, kind, j):
        src = (xs_send, xv_send)[kind].at[side, pl.ds(CHUNK * j, CHUNK)]
        dev = (s, j if side == 0 else 5 + j, ty)
        return remote(src, rel.at[kind], x_ss.at[side, kind, j], rel_rs.at[kind], dev)

    def relay_on(side, kind):
        j = tx if side == 0 else tx - 5
        dst = (xs_recv, xv_recv)[kind].at[side, pl.ds(CHUNK * j, CHUNK)]
        dev = (s, 4 if side == 0 else 3, ty)
        return remote(rel.at[kind], dst, rel_ss.at[kind], x_rs.at[side, kind, j], dev)

    near = (near_r, near_l)
    far = (is3, is4)
    exists_recv = (has_l, has_r)

    def send_x(kind):
        for side in range(2):
            @pl.when(far[side])
            def _():
                for j in range(3):
                    to_relay(side, kind, j).start()

            @pl.when(near[side])
            def _():
                for j in range(3):
                    x_copy(side, kind, j).start()

    exists_send_y = (upper, lower)
    exists_recv_y = (lower, upper)

    def y_copies(side):
        dev = (s, tx, ty + 1 if side == 0 else ty - 1)
        got = [remote(ysend.at[side], yrecv.at[side], y_ss.at[side, 0], y_rs.at[side, 0], dev)]
        for e in range(2):
            got.append(
                remote(bysend.at[side, e], byrecv.at[side, e], y_ss.at[side, 1 + e], y_rs.at[side, 1 + e], dev)
            )
        return got

    def y2_copy(side):
        dev = (s, tx, ty + 1 if side == 0 else ty - 1)
        src, dst = ((y2sb, y2rb), (y2sa, y2ra))[side]
        return remote(src, dst, y_ss.at[side, 3], y_rs.at[side, 3], dev)

    send_x(0)
    for side in range(2):
        @pl.when(exists_send_y[side])
        def _():
            for c in y_copies(side):
                c.start()

    relays = (low_relay, high_relay)
    for side in range(2):
        @pl.when(relays[side])
        def _():
            for kind in range(2):
                cp = relay_on(side, kind)
                to_relay(side, kind, 0).wait_recv()
                cp.start()

    for c in copies[7:]:
        c.wait()
    for side in range(2):
        @pl.when(exists_recv_y[side])
        def _():
            for c in y_copies(side):
                c.wait_recv()

    for w in range(2):
        k = 7 * w
        ST[w, XY, 2:18, 6:8, :] = yrecv[0, :, k:k + 2, :]
        ST[w, YZ, 2:18, 6:8, :] = yrecv[0, :, k + 2:k + 4, :]
        ST[w, YY, 2:18, 7:8, :] = yrecv[0, :, k + 4:k + 5, :]
        k = 8 * w
        ST[w, XY, 2:18, 24:25, :] = yrecv[1, :, k:k + 1, :]
        ST[w, YZ, 2:18, 24:25, :] = yrecv[1, :, k + 1:k + 2, :]
        ST[w, YY, 2:18, 24:26, :] = yrecv[1, :, k + 2:k + 4, :]

    zi = lax.broadcasted_iota(jnp.int32, (1, 1, 128), 2)
    up1 = (zi < 127).astype(F32)
    up2 = (zi < 126).astype(F32)
    dn1 = (zi > 0).astype(F32)
    dn2 = (zi > 1).astype(F32)

    def dpz(f):
        return (
            (C1 * up1) * pltpu.roll(f, 127, 2) - C1 * f
            + (C2 * up2) * pltpu.roll(f, 126, 2) - (C2 * dn1) * pltpu.roll(f, 1, 2)
        )

    def dmz(f):
        return (
            C1 * f - (C1 * dn1) * pltpu.roll(f, 1, 2)
            + (C2 * up1) * pltpu.roll(f, 127, 2) - (C2 * dn2) * pltpu.roll(f, 2, 2)
        )

    def getter(ref, w, x0, n):
        def get(c, dx=0, dy=0):
            return ref[w, c, pl.ds(2 + x0 + dx, n), 8 + dy:24 + dy, :]

        def dpx(c):
            return C1 * (get(c, 1) - get(c)) + C2 * (get(c, 2) - get(c, -1))

        def dmx(c):
            return C1 * (get(c) - get(c, -1)) + C2 * (get(c, 1) - get(c, -2))

        def dpy(c):
            return C1 * (get(c, 0, 1) - get(c)) + C2 * (get(c, 0, 2) - get(c, 0, -1))

        def dmy(c):
            return C1 * (get(c) - get(c, 0, -1)) + C2 * (get(c, 0, 1) - get(c, 0, -2))

        return get, dpx, dmx, dpy, dmy

    def accelerate(x0, n):
        scale = BU[pl.ds(2 + x0, n), 8:24, :]
        for w in range(2):
            get, dpx, dmx, dpy, dmy = getter(ST, w, x0, n)
            sums = (
                dpx(XX) + dmy(XY) + dmz(get(XZ)),
                dmx(XY) + dpy(YY) + dmz(get(YZ)),
                dmx(XZ) + dmy(YZ) + dpz(get(ZZ)),
            )
            for c in range(3):
                step = scale * sums[c]
                if w == 0:
                    AC[c, pl.ds(x0, n)] = step
                VE[w, c, pl.ds(2 + x0, n), 8:24, :] = VO[w, c, pl.ds(x0, n)] + step

    def accel_rows(i, carry):
        accelerate(2 * i, 2)
        return carry

    lax.fori_loop(0, 8, accel_rows, 0)

    for w in range(2):
        for i, (c, x) in enumerate([(0, 14), (0, 15), (1, 15), (2, 15)]):
            xv_send[0, 4 * w + i] = VE[w, c, 2 + x, 8:24, :]
        for i, (c, x) in enumerate([(0, 0), (1, 0), (1, 1), (2, 0), (2, 1)]):
            xv_send[1, 5 * w + i] = VE[w, c, 2 + x, 8:24, :]
        items = (
            [(XX, 15), (XY, 14), (XY, 15), (XZ, 14), (XZ, 15)],
            [(XX, 0), (XX, 1), (XY, 0), (XZ, 0)],
        )
        where = {XX: (5, 1, 4, 2), XY: (0, 2, 0, 1), XZ: (6, 1, 6, 2)}
        for side in range(2):
            for i, (c, x) in enumerate(items[side]):
                kb, nb, ka, na = where[c]
                xv_send[side, 10 + w, 3 * i:3 * i + nb, :] = yrecv[0, x, 7 * w + kb:7 * w + kb + nb, :]
                xv_send[side, 10 + w, 3 * i + nb:3 * i + 3, :] = yrecv[1, x, 8 * w + ka:8 * w + ka + na, :]
    send_x(1)
    for w in range(2):
        k = 4 * w
        for c, y, n in ((0, 15, 1), (1, 14, 2), (2, 15, 1)):
            y2sb[:, k:k + n, :] = VE[w, c, 2:18, 8 + y:8 + y + n, :]
            k += n
        k = 5 * w
        for c, y, n in ((0, 0, 2), (1, 0, 1), (2, 0, 2)):
            y2sa[:, k:k + n, :] = VE[w, c, 2:18, 8 + y:8 + y + n, :]
            k += n
    for side in range(2):
        @pl.when(exists_send_y[side])
        def _():
            y2_copy(side).start()
    for side in range(2):
        @pl.when(exists_recv_y[side])
        def _():
            y2_copy(side).wait_recv()
    for w in range(2):
        k = 4 * w
        for c, n in ((0, 1), (1, 2), (2, 1)):
            VE[w, c, 2:18, 8 - n:8, :] = y2rb[:, k:k + n, :]
            k += n
        k = 5 * w
        for c, n in ((0, 2), (1, 1), (2, 2)):
            VE[w, c, 2:18, 24:24 + n, :] = y2ra[:, k:k + n, :]
            k += n

    def finish(x0, n):
        lam = DT * LM[pl.ds(x0, n)]
        mu = DT * MU[pl.ds(x0, n)]
        rows = pl.ds(x0, n)
        kept = None
        for w, out in ((0, f_out), (1, a_out)):
            get, dpx, dmx, dpy, dmy = getter(VE, w, x0, n)
            vx, vy, vz = get(0), get(1), get(2)
            e = [
                dmx(0), dmy(1), dmz(vz),
                dpy(0) + dpx(1), dpz(vx) + dpx(2), dpz(vy) + dpy(2),
            ]
            trace = e[0] + e[1] + e[2]
            lt = lam * trace
            new = []
            for c in range(6):
                old = ST[w, c, pl.ds(2 + x0, n), 8:24, :]
                new.append(old + (lt + (2.0 * mu) * e[c]) if c < 3 else old + mu * e[c])
                out[3 + c, rows] = new[c]
            for c, v in enumerate((vx, vy, vz)):
                out[c, rows] = v
            if w == 0:
                kept = (trace, e)
            else:
                trace0, e0 = kept
                GL[0, rows] = (-DT) * trace0 * (new[0] + new[1] + new[2])
                prod = e0[0] * new[0]
                for c in range(1, 6):
                    prod = prod + e0[c] * new[c]
                GL[1, rows] = (-DT) * prod
                GL[2, rows] = -(AC[0, rows] * vx + AC[1, rows] * vy + AC[2, rows] * vz)

    def g_copy(k):
        lo, n = ((4, 8), (0, 4), (12, 4))[k]
        return remote(
            GL.at[:, pl.ds(lo, n)], GR.at[:, pl.ds(lo, n)], g_ss.at[k], g_rs.at[k], partner
        )

    def finish_rows(i, carry):
        finish(2 * i, 2)
        return carry

    lax.fori_loop(2, 6, finish_rows, 0)
    g_copy(0).start()

    def correct(w, c, x, e, terms):
        nb = 2 if c == 1 else 1
        layer, side = 10 + w, e
        lower_part = sum(k * xv_recv[side, layer, 3 * i:3 * i + nb, :] for i, k in terms)
        upper_part = sum(k * xv_recv[side, layer, 3 * i + nb:3 * i + 3, :] for i, k in terms)
        r = x if e == 0 else x - 14
        VE[w, c, 2 + x, 8 - nb:8, :] = VE[w, c, 2 + x, 8 - nb:8, :] + byrecv[0, e, r, 8 - nb:8, :] * lower_part
        na = 3 - nb
        VE[w, c, 2 + x, 24:24 + na, :] = VE[w, c, 2 + x, 24:24 + na, :] + byrecv[1, e, r, 0:na, :] * upper_part

    def edge(side):
        @pl.when(exists_recv[side])
        def _():
            for kind in range(2):
                for j in range(3):
                    x_copy(side, kind, j).wait_recv()

        def mine(w, c, x):
            return ST[w, c, 2 + x, 8:24, :]

        if side == 0:
            b2, b1 = xs_recv[0, 10], xs_recv[0, 11]
            for w in range(2):
                k = 5 * w
                ST[w, XX, 1, 8:24, :] = xs_recv[0, k]
                ST[w, XY, 0:2, 8:24, :] = xs_recv[0, k + 1:k + 3]
                ST[w, XZ, 0:2, 8:24, :] = xs_recv[0, k + 3:k + 5]
                k = 4 * w
                VE[w, 0, 0, 8:24, :] = xv_recv[0, k] + b2 * (C2 * mine(w, XX, 0))
                VE[w, 0, 1, 8:24, :] = xv_recv[0, k + 1] + b1 * (C1 * mine(w, XX, 0) + C2 * mine(w, XX, 1))
                VE[w, 1, 1, 8:24, :] = xv_recv[0, k + 2] + b1 * (C2 * mine(w, XY, 0))
                VE[w, 2, 1, 8:24, :] = xv_recv[0, k + 3] + b1 * (C2 * mine(w, XZ, 0))
                correct(w, 0, 0, 0, ((0, -C2),))
                correct(w, 1, 0, 0, ((2, -C1), (1, -C2)))
                correct(w, 1, 1, 0, ((2, -C2),))
                correct(w, 2, 0, 0, ((4, -C1), (3, -C2)))
                correct(w, 2, 1, 0, ((4, -C2),))
            accelerate(0, 2)
            first = 0
        else:
            b1, b2 = xs_recv[1, 8], xs_recv[1, 9]
            for w in range(2):
                k = 4 * w
                ST[w, XX, 18:20, 8:24, :] = xs_recv[1, k:k + 2]
                ST[w, XY, 18, 8:24, :] = xs_recv[1, k + 2]
                ST[w, XZ, 18, 8:24, :] = xs_recv[1, k + 3]
                k = 5 * w
                VE[w, 0, 18, 8:24, :] = xv_recv[1, k] - b1 * (C2 * mine(w, XX, 15))
                for c, st, at in ((1, XY, k + 1), (2, XZ, k + 3)):
                    VE[w, c, 18, 8:24, :] = xv_recv[1, at] - b1 * (C1 * mine(w, st, 15) + C2 * mine(w, st, 14))
                    VE[w, c, 19, 8:24, :] = xv_recv[1, at + 1] - b2 * (C2 * mine(w, st, 15))
                correct(w, 0, 14, 1, ((0, C2),))
                correct(w, 0, 15, 1, ((0, C1), (1, C2)))
                correct(w, 1, 15, 1, ((2, C2),))
                correct(w, 2, 15, 1, ((3, C2),))
            accelerate(14, 2)
            first = 6

        lax.fori_loop(first, first + 2, finish_rows, 0)
        g_copy(1 + side).start()

    @pl.when(jnp.logical_not(is4))
    def _():
        edge(0)

    edge(1)

    @pl.when(is4)
    def _():
        edge(0)

    for k, (lo, n) in enumerate(((4, 8), (0, 4), (12, 4))):
        g_copy(k).wait_recv()
        for c in range(3):
            g_out[c, lo:lo + n] = GL[c, lo:lo + n] + GR[c, lo:lo + n]

    for k in range(3):
        g_copy(k).wait_send()
    for side in range(2):
        @pl.when(exists_send_y[side])
        def _():
            for c in y_copies(side):
                c.wait_send()
            y2_copy(side).wait_send()

        @pl.when(near[side] | far[side])
        def _():
            for kind in range(2):
                for j in range(3):
                    x_copy(side, kind, j).wait_send()

        @pl.when(relays[side])
        def _():
            for kind in range(2):
                relay_on(side, kind).wait_send()


def store_kernel(f, a, g, f_out, a_out, g_out, sem):
    copies = [
        pltpu.make_async_copy(src, dst, sem.at[i])
        for i, (src, dst) in enumerate(((f, f_out), (a, a_out), (g, g_out)))
    ]
    for c in copies:
        c.start()
    for c in copies:
        c.wait()


def body(fwd, adj, lam, mu, den, scell, samp, rcell, ramp):
    fields, grads = (9, 16, 16, 128), (3, 16, 16, 128)
    hbm = pl.BlockSpec(memory_space=pltpu.HBM)
    vmem = pl.BlockSpec(memory_space=pltpu.VMEM)
    dma = pltpu.SemaphoreType.DMA

    def buf(*shape, dtype=F32):
        return pltpu.VMEM(shape, dtype)

    f, a, g = pl.pallas_call(
        step_kernel,
        out_shape=(pltpu.VMEM(fields, F32), pltpu.VMEM(fields, F32), pltpu.VMEM(grads, F32)),
        in_specs=[hbm] * 9,
        out_specs=(vmem, vmem, vmem),
        scratch_shapes=[
            buf(2, 6, 20, 32, 128), buf(2, 3, 20, 32, 128), buf(2, 3, 16, 16, 128), buf(3, 16, 16, 128),
            buf(20, 32, 128), buf(16, 16, 128), buf(16, 16, 128), buf(16, 16, 128),
            buf(1, 256, dtype=jnp.int32), buf(1, 256),
            pltpu.SMEM((1,), jnp.int32), pltpu.SMEM((1,), F32),
            buf(2, 16, 16, 128), buf(2, 16, 16, 128), buf(2, 2, 2, 8, 128), buf(2, 2, 2, 8, 128),
            buf(16, 8, 128), buf(16, 16, 128), buf(16, 8, 128), buf(16, 16, 128),
            buf(2, 12, 16, 128), buf(2, 12, 16, 128), buf(2, 12, 16, 128), buf(2, 12, 16, 128),
            buf(2, CHUNK, 16, 128), buf(3, 16, 16, 128), buf(3, 16, 16, 128),
            dma((11,)), dma((2, 4)), dma((2, 4)), dma((2, 2, 3)), dma((2, 2, 3)),
            dma((2,)), dma((2,)), dma((3,)), dma((3,)),
        ],
        compiler_params=pltpu.CompilerParams(
            collective_id=1, has_side_effects=True, vmem_limit_bytes=56 * 1024 * 1024
        ),
        name="step",
    )(fwd, adj, lam, mu, den, scell, samp, rcell, ramp)
    f, a, g = pl.pallas_call(
        store_kernel,
        out_shape=tuple(jax.ShapeDtypeStruct(shape, F32) for shape in (fields, fields, grads)),
        in_specs=[vmem] * 3,
        out_specs=(hbm,) * 3,
        scratch_shapes=[dma((3,))],
        compiler_params=pltpu.CompilerParams(vmem_limit_bytes=16 * 1024 * 1024),
        name="store",
    )(f, a, g)
    return f[None], a[None], g


def solution(mesh):
    fields = P("shot", None, "tx", "ty", None)
    grid = P("tx", "ty", None)
    return jax.shard_map(
        body,
        mesh=mesh,
        in_specs=(fields, fields, grid, grid, grid, P("shot"), P("shot"), P("shot", None), P("shot", None)),
        out_specs=(fields, fields, P(None, "tx", "ty", None)),
        check_vma=False,
    )
```

```python
import functools

import jax
import jax.numpy as jnp
from jax import lax
from jax.experimental import pallas as pl
from jax.experimental.pallas import tpu as pltpu
from jax.sharding import PartitionSpec as P

C1 = 9.0 / 8.0
C2 = -1.0 / 24.0
DT = 0.15
MESH = pl.DeviceIdType.MESH
F32 = jnp.float32
XX, YY, ZZ, XY, XZ, YZ = range(6)


def step_kernel(
    fwd, adj, lam_h, mu_h, den_h, source_h, rcell_h, ramp_h,
    f_out, a_out, g_out,
    ST, VE, VO, AC, BU, LM, MU, ADD, rcell, ramp, source,
    ysend, yrecv, bysend, byrecv, y2sb, y2sa, y2rb, y2ra,
    xs_send, xv_send, xe_send, xs_recv, xv_recv, xe_recv, rel_s, rel_v, GL, GR,
    in_sem, y_ss, y_rs, x_ss, x_rs, rel_ss, rel_rs, g_ss, g_rs,
):
    s, tx, ty = lax.axis_index("shot"), lax.axis_index("tx"), lax.axis_index("ty")
    last = lax.axis_size("ty") - 1
    partner = (1 - s, tx, ty)

    near_l, near_r = (tx > 0) & (tx != 4), (tx < 7) & (tx != 3)
    lower, upper = ty > 0, ty < last
    is3, is4 = tx == 3, tx == 4
    low_relay, high_relay = tx < 3, tx > 4

    bar = pltpu.get_barrier_semaphore()

    def greet(cond, dev):
        @pl.when(cond)
        def _():
            pl.semaphore_signal(bar, inc=1, device_id=dev, device_id_type=MESH)

    greet(is3, (s, 4, ty))
    greet(is4, (s, 3, ty))
    greet(lower, (s, tx, ty - 1))
    greet(upper, (s, tx, ty + 1))
    greet(near_l, (s, tx - 1, ty))
    greet(near_r, (s, tx + 1, ty))
    greet(tx < 2, (s, 3, ty))
    greet(tx > 5, (s, 4, ty))
    pl.semaphore_signal(bar, inc=1, device_id=partner, device_id_type=MESH)

    loads = [
        (fwd.at[0, pl.ds(3, 6)], ST.at[0, :, pl.ds(2, 16), pl.ds(8, 16)]),
        (adj.at[0, pl.ds(3, 6)], ST.at[1, :, pl.ds(2, 16), pl.ds(8, 16)]),
        (rcell_h, rcell),
        (ramp_h, ramp),
        (source_h, source),
        (den_h, BU.at[pl.ds(2, 16), pl.ds(8, 16)]),
        (fwd.at[0, pl.ds(0, 3)], VO.at[0]),
        (adj.at[0, pl.ds(0, 3)], VO.at[1]),
        (lam_h, LM),
        (mu_h, MU),
    ]
    copies = [pltpu.make_async_copy(a, b, in_sem.at[i]) for i, (a, b) in enumerate(loads)]
    for c in copies:
        c.start()

    def clear(cond, ref, idx):
        @pl.when(cond)
        def _():
            ref[idx] = jnp.zeros(ref.at[idx].shape, F32)

    for w in range(2):
        for c in (XX, XY, XZ):
            for lo in (0, 18):
                ST[w, c, lo:lo + 2, 8:24, :] = jnp.zeros((2, 16, 128), F32)
    for side, gone in ((0, ty == 0), (1, ty == last)):
        clear(gone, yrecv, side)
        clear(gone, byrecv, side)
    clear(ty == 0, y2rb, slice(None))
    clear(ty == last, y2ra, slice(None))
    for side, gone in ((0, tx == 0), (1, tx == 7)):
        clear(gone, xs_recv, side)
        clear(gone, xv_recv, side)
        clear(gone, xe_recv, side)
    xe_send[...] = jnp.zeros(xe_send.shape, F32)
    for w in range(2):
        for c in (XY, YY, YZ):
            for lo in (0, 24):
                ST[w, c, 2:18, lo:lo + 8, :] = jnp.zeros((16, 8, 128), F32)
    ysend[0, :, 8:16, :] = jnp.zeros((16, 8, 128), F32)
    y2sa[:, 8:16, :] = jnp.zeros((16, 8, 128), F32)

    for c in copies[2:5]:
        c.wait()

    def place(cell):
        lx = (cell >> 16) - tx * 16
        ly = ((cell >> 7) & 511) - ty * 16
        inside = (lx >= 0) & (lx < 16) & (ly >= 0) & (ly < 16)
        return jnp.where(inside, lx * 16 + ly, -1), cell & 127

    column, depth = place(rcell[...])
    hot = (lax.broadcasted_iota(jnp.int32, (256, 256), 0) == column).astype(jnp.bfloat16)
    amount = jnp.where(lax.broadcasted_iota(jnp.int32, (128, 256), 0) == depth, ramp[...], 0.0)
    high = amount.astype(jnp.bfloat16)
    rest = amount - high.astype(F32)
    mid = rest.astype(jnp.bfloat16)
    low = (rest - mid.astype(F32)).astype(jnp.bfloat16)
    nt = (((1,), (1,)), ((), ()))
    added = sum(
        lax.dot_general(hot, part, nt, preferred_element_type=F32) for part in (low, mid, high)
    )
    ADD[...] = added.reshape(16, 16, 128)
    copies[0].wait()
    copies[1].wait()

    def inject_rows(i, carry):
        shape = (2, 16, 128)
        gx = lax.broadcasted_iota(jnp.int32, shape, 0) + (2 * i + tx * 16)
        gy = lax.broadcasted_iota(jnp.int32, shape, 1) + ty * 16
        cell = gx * 65536 + gy * 128 + lax.broadcasted_iota(jnp.int32, shape, 2)
        src = jnp.where(cell.astype(F32) == source[0], source[1], 0.0)
        rows = pl.ds(2 + 2 * i, 2)
        for c in range(3):
            ST[0, c, rows, 8:24, :] = ST[0, c, rows, 8:24, :] + src
            ST[1, c, rows, 8:24, :] = ST[1, c, rows, 8:24, :] + ADD[pl.ds(2 * i, 2)]
        return carry

    lax.fori_loop(0, 8, inject_rows, 0)
    copies[5].wait()
    BU[2:18, 8:24, :] = DT / BU[2:18, 8:24, :]

    for w in range(2):
        layers = [(XX, 15), (XY, 14), (XY, 15), (XZ, 14), (XZ, 15)]
        for i, (c, x) in enumerate(layers):
            xs_send[0, 5 * w + i] = ST[w, c, 2 + x, 8:24, :]
        layers = [(XX, 0), (XX, 1), (XY, 0), (XZ, 0)]
        for i, (c, x) in enumerate(layers):
            xs_send[1, 4 * w + i] = ST[w, c, 2 + x, 8:24, :]
    for i in range(2):
        xv_send[0, 8 + i] = BU[16 + i, 8:24, :]
        xs_send[1, 8 + i] = BU[2 + i, 8:24, :]
    for w in range(2):
        rows = [(XY, 14, 2), (YZ, 14, 2), (YY, 15, 1), (XX, 15, 1), (XZ, 15, 1)]
        k = 7 * w
        for c, y, n in rows:
            ysend[0, :, k:k + n, :] = ST[w, c, 2:18, 8 + y:8 + y + n, :]
            k += n
        rows = [(XY, 0, 1), (YZ, 0, 1), (YY, 0, 2), (XX, 0, 2), (XZ, 0, 2)]
        k = 8 * w
        for c, y, n in rows:
            ysend[1, :, k:k + n, :] = ST[w, c, 2:18, 8 + y:8 + y + n, :]
            k += n
    for e, x in ((0, 0), (1, 14)):
        bysend[0, e] = BU[2 + x:4 + x, 16:24, :]
        bysend[1, e] = BU[2 + x:4 + x, 8:16, :]

    zi = lax.broadcasted_iota(jnp.int32, (1, 1, 128), 2)
    up1 = (zi < 127).astype(F32)
    up2 = (zi < 126).astype(F32)
    dn1 = (zi > 0).astype(F32)
    dn2 = (zi > 1).astype(F32)

    def dpz(f):
        return (
            (C1 * up1) * pltpu.roll(f, 127, 2) - C1 * f
            + (C2 * up2) * pltpu.roll(f, 126, 2) - (C2 * dn1) * pltpu.roll(f, 1, 2)
        )

    def dmz(f):
        return (
            C1 * f - (C1 * dn1) * pltpu.roll(f, 1, 2)
            + (C2 * up1) * pltpu.roll(f, 127, 2) - (C2 * dn2) * pltpu.roll(f, 2, 2)
        )

    def getter(ref, w, x0, n):
        def get(c, dx=0, dy=0):
            return ref[w, c, pl.ds(2 + x0 + dx, n), 8 + dy:24 + dy, :]

        def dpx(c):
            return C1 * (get(c, 1) - get(c)) + C2 * (get(c, 2) - get(c, -1))

        def dmx(c):
            return C1 * (get(c) - get(c, -1)) + C2 * (get(c, 1) - get(c, -2))

        def dpy(c):
            return C1 * (get(c, 0, 1) - get(c)) + C2 * (get(c, 0, 2) - get(c, 0, -1))

        def dmy(c):
            return C1 * (get(c) - get(c, 0, -1)) + C2 * (get(c, 0, 1) - get(c, 0, -2))

        return get, dpx, dmx, dpy, dmy

    def accelerate(x0, n):
        scale = BU[pl.ds(2 + x0, n), 8:24, :]
        for w in range(2):
            get, dpx, dmx, dpy, dmy = getter(ST, w, x0, n)
            sums = (
                dpx(XX) + dmy(XY) + dmz(get(XZ)),
                dmx(XY) + dpy(YY) + dmz(get(YZ)),
                dmx(XZ) + dmy(YZ) + dpz(get(ZZ)),
            )
            for c in range(3):
                step = scale * sums[c]
                if w == 0:
                    AC[c, pl.ds(x0, n)] = step
                VE[w, c, pl.ds(2 + x0, n), 8:24, :] = VO[w, c, pl.ds(x0, n)] + step

    for c in copies[6:]:
        c.wait()
    accelerate(0, 2)
    accelerate(14, 2)

    for w in range(2):
        for i, (c, x) in enumerate([(0, 14), (0, 15), (1, 15), (2, 15)]):
            xv_send[0, 4 * w + i] = VE[w, c, 2 + x, 8:24, :]
        for i, (c, x) in enumerate([(0, 0), (1, 0), (1, 1), (2, 0), (2, 1)]):
            xv_send[1, 5 * w + i] = VE[w, c, 2 + x, 8:24, :]

    def one(cond):
        return jnp.where(cond, 1, 0)

    far_end = is3 | is4
    peers = 1 + one(lower) + one(upper) + one(near_l) + one(near_r) + 3 * one(far_end)
    pl.semaphore_wait(bar, peers)

    def remote(src, dst, ss, rs, dev):
        return pltpu.make_async_remote_copy(
            src_ref=src, dst_ref=dst, send_sem=ss, recv_sem=rs, device_id=dev, device_id_type=MESH
        )

    x_send = (xs_send, xv_send, xe_send)
    x_recv = (xs_recv, xv_recv, xe_recv)
    relay_buf = (rel_s, rel_v)

    def layers_of(kind, j):
        if j is None:
            return (pl.ds(0, 4), pl.ds(9, 1))[kind]
        return (pl.ds(4 + 2 * j, 2), pl.ds(3 * j, 3))[kind]

    def x_near(side, kind):
        dev = (s, tx + 1 if side == 0 else tx - 1, ty)
        return remote(
            x_send[kind].at[side], x_recv[kind].at[side], x_ss.at[side, kind, 0], x_rs.at[side, kind, 0], dev
        )

    def x_straight(side, kind):
        dev = (s, 4 if side == 0 else 3, ty)
        part = layers_of(kind, None)
        return remote(
            x_send[kind].at[side, part], x_recv[kind].at[side, part],
            x_ss.at[side, kind, 0], x_rs.at[side, kind, 0], dev,
        )

    def to_relay(side, kind, j):
        dev = (s, j if side == 0 else 5 + j, ty)
        return remote(
            x_send[kind].at[side, layers_of(kind, j)], relay_buf[kind],
            x_ss.at[side, kind, 1 + j], rel_rs.at[kind], dev,
        )

    def relay_on(side, kind, j):
        dev = (s, 4 if side == 0 else 3, ty)
        return remote(
            relay_buf[kind], x_recv[kind].at[side, layers_of(kind, j)],
            rel_ss.at[kind], x_rs.at[side, kind, 1 + j], dev,
        )

    near = (near_r, near_l)
    far = (is3, is4)
    near_recv = (near_l, near_r)
    far_recv = (is4, is3)

    def far_copies(side, kind):
        if kind == 2:
            return [x_near(side, 2)]
        return [to_relay(side, kind, j) for j in range(3)] + [x_straight(side, kind)]

    def send_x(kind):
        for side in range(2):
            @pl.when(far[side])
            def _():
                for cp in far_copies(side, kind):
                    cp.start()

            @pl.when(near[side])
            def _():
                x_near(side, kind).start()

    exists_send_y = (upper, lower)
    exists_recv_y = (lower, upper)

    def y_copies(side):
        dev = (s, tx, ty + 1 if side == 0 else ty - 1)
        got = [remote(ysend.at[side], yrecv.at[side], y_ss.at[side, 0], y_rs.at[side, 0], dev)]
        for e in range(2):
            got.append(
                remote(bysend.at[side, e], byrecv.at[side, e], y_ss.at[side, 1 + e], y_rs.at[side, 1 + e], dev)
            )
        return got

    def y2_copy(side):
        dev = (s, tx, ty + 1 if side == 0 else ty - 1)
        src, dst = ((y2sb, y2rb), (y2sa, y2ra))[side]
        return remote(src, dst, y_ss.at[side, 3], y_rs.at[side, 3], dev)

    send_x(0)
    send_x(1)
    for side in range(2):
        @pl.when(exists_send_y[side])
        def _():
            for c in y_copies(side):
                c.start()


    for side in range(2):
        @pl.when(exists_recv_y[side])
        def _():
            for c in y_copies(side):
                c.wait_recv()

    for w in range(2):
        k = 7 * w
        ST[w, XY, 2:18, 6:8, :] = yrecv[0, :, k:k + 2, :]
        ST[w, YZ, 2:18, 6:8, :] = yrecv[0, :, k + 2:k + 4, :]
        ST[w, YY, 2:18, 7:8, :] = yrecv[0, :, k + 4:k + 5, :]
        k = 8 * w
        ST[w, XY, 2:18, 24:25, :] = yrecv[1, :, k:k + 1, :]
        ST[w, YZ, 2:18, 24:25, :] = yrecv[1, :, k + 1:k + 2, :]
        ST[w, YY, 2:18, 24:26, :] = yrecv[1, :, k + 2:k + 4, :]

    items = (
        [(XX, 15), (XY, 14), (XY, 15), (XZ, 14), (XZ, 15), (YY, 15), (YZ, 15)],
        [(XX, 0), (XX, 1), (XY, 0), (XZ, 0), (YY, 0), (YY, 1), (YZ, 0), (YZ, 1)],
    )
    where = {XX: (5, 1, 4, 2), XY: (0, 2, 0, 1), XZ: (6, 1, 6, 2), YY: (4, 1, 2, 2), YZ: (2, 2, 1, 1)}
    for side in range(2):
        for w in range(2):
            for i, (c, x) in enumerate(items[side]):
                kb, nb, ka, na = where[c]
                xe_send[side, w, 3 * i:3 * i + nb, :] = yrecv[0, x, 7 * w + kb:7 * w + kb + nb, :]
                xe_send[side, w, 3 * i + nb:3 * i + 3, :] = yrecv[1, x, 8 * w + ka:8 * w + ka + na, :]
    send_x(2)

    def accel_rows(i, carry):
        accelerate(2 * i, 2)
        return carry

    lax.fori_loop(0, 8, accel_rows, 0)

    for w in range(2):
        k = 4 * w
        for c, y, n in ((0, 15, 1), (1, 14, 2), (2, 15, 1)):
            y2sb[:, k:k + n, :] = VE[w, c, 2:18, 8 + y:8 + y + n, :]
            k += n
        k = 5 * w
        for c, y, n in ((0, 0, 2), (1, 0, 1), (2, 0, 2)):
            y2sa[:, k:k + n, :] = VE[w, c, 2:18, 8 + y:8 + y + n, :]
            k += n
    for side in range(2):
        @pl.when(exists_send_y[side])
        def _():
            y2_copy(side).start()
    relays = (low_relay, high_relay)
    for side in range(2):
        @pl.when(relays[side])
        def _():
            j = tx if side == 0 else tx - 5
            for kind in range(2):
                to_relay(side, kind, 0).wait_recv()
                relay_on(side, kind, j).start()

    for side in range(2):
        @pl.when(exists_recv_y[side])
        def _():
            y2_copy(side).wait_recv()
    for w in range(2):
        k = 4 * w
        for c, n in ((0, 1), (1, 2), (2, 1)):
            VE[w, c, 2:18, 8 - n:8, :] = y2rb[:, k:k + n, :]
            k += n
        k = 5 * w
        for c, n in ((0, 2), (1, 1), (2, 2)):
            VE[w, c, 2:18, 24:24 + n, :] = y2ra[:, k:k + n, :]
            k += n

    def finish(x0, n):
        lam = DT * LM[pl.ds(x0, n)]
        mu = DT * MU[pl.ds(x0, n)]
        rows = pl.ds(x0, n)
        kept = None
        for w, out in ((0, f_out), (1, a_out)):
            get, dpx, dmx, dpy, dmy = getter(VE, w, x0, n)
            vx, vy, vz = get(0), get(1), get(2)
            e = [
                dmx(0), dmy(1), dmz(vz),
                dpy(0) + dpx(1), dpz(vx) + dpx(2), dpz(vy) + dpy(2),
            ]
            trace = e[0] + e[1] + e[2]
            lt = lam * trace
            new = []
            for c in range(6):
                old = ST[w, c, pl.ds(2 + x0, n), 8:24, :]
                new.append(old + (lt + (2.0 * mu) * e[c]) if c < 3 else old + mu * e[c])
                out[3 + c, rows] = new[c]
            for c, v in enumerate((vx, vy, vz)):
                out[c, rows] = v
            if w == 0:
                kept = (trace, e)
            else:
                trace0, e0 = kept
                GL[0, rows] = (-DT) * trace0 * (new[0] + new[1] + new[2])
                prod = e0[0] * new[0]
                for c in range(1, 6):
                    prod = prod + e0[c] * new[c]
                GL[1, rows] = (-DT) * prod
                GL[2, rows] = -(AC[0, rows] * vx + AC[1, rows] * vy + AC[2, rows] * vz)

    def g_copy(k):
        lo, n = ((4, 8), (0, 4), (12, 4))[k]
        return remote(
            GL.at[:, pl.ds(lo, n)], GR.at[:, pl.ds(lo, n)], g_ss.at[k], g_rs.at[k], partner
        )

    def finish_rows(i, carry):
        finish(2 * i, 2)
        return carry

    lax.fori_loop(2, 6, finish_rows, 0)
    g_copy(0).start()

    def correct(w, c, x, e, terms):
        nb = 2 if c == 1 else 1
        lower_part = sum(k * xe_recv[e, w, 3 * i:3 * i + nb, :] for i, k in terms)
        upper_part = sum(k * xe_recv[e, w, 3 * i + nb:3 * i + 3, :] for i, k in terms)
        r = x if e == 0 else x - 14
        VE[w, c, 2 + x, 8 - nb:8, :] = VE[w, c, 2 + x, 8 - nb:8, :] + byrecv[0, e, r, 8 - nb:8, :] * lower_part
        na = 3 - nb
        VE[w, c, 2 + x, 24:24 + na, :] = VE[w, c, 2 + x, 24:24 + na, :] + byrecv[1, e, r, 0:na, :] * upper_part

    def rim(w, c, x, e, scale, i, forward):
        def f(k):
            return xe_recv[e, w, 3 * i + k:3 * i + k + 1, :]

        if forward:
            adds = ((0, -C2 * f(0)), (14, C2 * f(1)), (15, C1 * f(1) + C2 * f(2)))
        else:
            adds = ((0, -C1 * f(1) - C2 * f(0)), (1, -C2 * f(1)), (15, C2 * f(2)))
        for y, v in adds:
            VE[w, c, x, 8 + y:9 + y, :] = VE[w, c, x, 8 + y:9 + y, :] + scale[y:y + 1, :] * v

    def edge(side):
        @pl.when(near_recv[side])
        def _():
            for kind in range(3):
                x_near(side, kind).wait_recv()

        @pl.when(far_recv[side])
        def _():
            for kind in range(2):
                for j in range(3):
                    relay_on(side, kind, j).wait_recv()
                x_straight(side, kind).wait_recv()
            x_near(side, 2).wait_recv()

        def mine(w, c, x):
            return ST[w, c, 2 + x, 8:24, :]

        if side == 0:
            b2, b1 = xv_recv[0, 8], xv_recv[0, 9]
            for w in range(2):
                k = 5 * w
                ST[w, XX, 1, 8:24, :] = xs_recv[0, k]
                ST[w, XY, 0:2, 8:24, :] = xs_recv[0, k + 1:k + 3]
                ST[w, XZ, 0:2, 8:24, :] = xs_recv[0, k + 3:k + 5]
                k = 4 * w
                VE[w, 0, 0, 8:24, :] = xv_recv[0, k] + b2 * (C2 * mine(w, XX, 0))
                VE[w, 0, 1, 8:24, :] = xv_recv[0, k + 1] + b1 * (C1 * mine(w, XX, 0) + C2 * mine(w, XX, 1))
                VE[w, 1, 1, 8:24, :] = xv_recv[0, k + 2] + b1 * (C2 * mine(w, XY, 0))
                VE[w, 2, 1, 8:24, :] = xv_recv[0, k + 3] + b1 * (C2 * mine(w, XZ, 0))
                rim(w, 0, 0, 0, xv_recv.at[0, 8], 1, False)
                rim(w, 0, 1, 0, xv_recv.at[0, 9], 2, False)
                rim(w, 1, 1, 0, xv_recv.at[0, 9], 5, True)
                rim(w, 2, 1, 0, xv_recv.at[0, 9], 6, False)
                correct(w, 0, 0, 0, ((0, -C2),))
                correct(w, 1, 0, 0, ((2, -C1), (1, -C2)))
                correct(w, 1, 1, 0, ((2, -C2),))
                correct(w, 2, 0, 0, ((4, -C1), (3, -C2)))
                correct(w, 2, 1, 0, ((4, -C2),))
            accelerate(0, 2)
            first = 0
        else:
            b1, b2 = xs_recv[1, 8], xs_recv[1, 9]
            for w in range(2):
                k = 4 * w
                ST[w, XX, 18:20, 8:24, :] = xs_recv[1, k:k + 2]
                ST[w, XY, 18, 8:24, :] = xs_recv[1, k + 2]
                ST[w, XZ, 18, 8:24, :] = xs_recv[1, k + 3]
                k = 5 * w
                VE[w, 0, 18, 8:24, :] = xv_recv[1, k] - b1 * (C2 * mine(w, XX, 15))
                for c, st, at in ((1, XY, k + 1), (2, XZ, k + 3)):
                    VE[w, c, 18, 8:24, :] = xv_recv[1, at] - b1 * (C1 * mine(w, st, 15) + C2 * mine(w, st, 14))
                    VE[w, c, 19, 8:24, :] = xv_recv[1, at + 1] - b2 * (C2 * mine(w, st, 15))
                rim(w, 0, 18, 1, xs_recv.at[1, 8], 2, False)
                rim(w, 1, 18, 1, xs_recv.at[1, 8], 4, True)
                rim(w, 1, 19, 1, xs_recv.at[1, 9], 5, True)
                rim(w, 2, 18, 1, xs_recv.at[1, 8], 6, False)
                rim(w, 2, 19, 1, xs_recv.at[1, 9], 7, False)
                correct(w, 0, 14, 1, ((0, C2),))
                correct(w, 0, 15, 1, ((0, C1), (1, C2)))
                correct(w, 1, 15, 1, ((2, C2),))
                correct(w, 2, 15, 1, ((3, C2),))
            accelerate(14, 2)
            first = 6

        lax.fori_loop(first, first + 2, finish_rows, 0)
        g_copy(1 + side).start()

    @pl.when(jnp.logical_not(is4))
    def _():
        edge(0)

    edge(1)

    @pl.when(is4)
    def _():
        edge(0)

    for k, (lo, n) in enumerate(((4, 8), (0, 4), (12, 4))):
        g_copy(k).wait_recv()
        for c in range(3):
            g_out[c, lo:lo + n] = GL[c, lo:lo + n] + GR[c, lo:lo + n]

    for k in range(3):
        g_copy(k).wait_send()
    for side in range(2):
        @pl.when(exists_send_y[side])
        def _():
            for c in y_copies(side):
                c.wait_send()
            y2_copy(side).wait_send()

        @pl.when(near[side])
        def _():
            for kind in range(3):
                x_near(side, kind).wait_send()

        @pl.when(far[side])
        def _():
            for kind in range(3):
                for cp in far_copies(side, kind):
                    cp.wait_send()

        @pl.when(relays[side])
        def _():
            for kind in range(2):
                relay_on(side, kind, 0).wait_send()


def store_kernel(f, a, g, f_out, a_out, g_out, sem):
    copies = [
        pltpu.make_async_copy(src, dst, sem.at[i])
        for i, (src, dst) in enumerate(((f, f_out), (a, a_out), (g, g_out)))
    ]
    for c in copies:
        c.start()
    for c in copies:
        c.wait()


def body(fwd, adj, lam, mu, den, scell, samp, rcell, ramp):
    fields, grads = (9, 16, 16, 128), (3, 16, 16, 128)
    hbm = pl.BlockSpec(memory_space=pltpu.HBM)
    vmem = pl.BlockSpec(memory_space=pltpu.VMEM)
    dma = pltpu.SemaphoreType.DMA

    source = jnp.concatenate([scell.astype(F32), samp])

    def buf(*shape, dtype=F32):
        return pltpu.VMEM(shape, dtype)

    f, a, g = pl.pallas_call(
        step_kernel,
        out_shape=(pltpu.VMEM(fields, F32), pltpu.VMEM(fields, F32), pltpu.VMEM(grads, F32)),
        in_specs=[hbm] * 8,
        out_specs=(vmem, vmem, vmem),
        scratch_shapes=[
            buf(2, 6, 20, 32, 128), buf(2, 3, 20, 32, 128), buf(2, 3, 16, 16, 128), buf(3, 16, 16, 128),
            buf(20, 32, 128), buf(16, 16, 128), buf(16, 16, 128), buf(16, 16, 128),
            buf(1, 256, dtype=jnp.int32), buf(1, 256),
            pltpu.SMEM((2,), F32),
            buf(2, 16, 16, 128), buf(2, 16, 16, 128), buf(2, 2, 2, 8, 128), buf(2, 2, 2, 8, 128),
            buf(16, 8, 128), buf(16, 16, 128), buf(16, 8, 128), buf(16, 16, 128),
            buf(2, 10, 16, 128), buf(2, 10, 16, 128), buf(2, 2, 24, 128),
            buf(2, 10, 16, 128), buf(2, 10, 16, 128), buf(2, 2, 24, 128),
            buf(2, 16, 128), buf(3, 16, 128), buf(3, 16, 16, 128), buf(3, 16, 16, 128),
            dma((10,)), dma((2, 4)), dma((2, 4)), dma((2, 3, 4)), dma((2, 3, 4)),
            dma((2,)), dma((2,)), dma((3,)), dma((3,)),
        ],
        compiler_params=pltpu.CompilerParams(
            collective_id=1, has_side_effects=True, vmem_limit_bytes=56 * 1024 * 1024
        ),
        name="step",
    )(fwd, adj, lam, mu, den, source, rcell, ramp)
    f, a, g = pl.pallas_call(
        store_kernel,
        out_shape=tuple(jax.ShapeDtypeStruct(shape, F32) for shape in (fields, fields, grads)),
        in_specs=[vmem] * 3,
        out_specs=(hbm,) * 3,
        scratch_shapes=[dma((3,))],
        compiler_params=pltpu.CompilerParams(vmem_limit_bytes=16 * 1024 * 1024),
        name="store",
    )(f, a, g)
    return f[None], a[None], g


def solution(mesh):
    fields = P("shot", None, "tx", "ty", None)
    grid = P("tx", "ty", None)
    return jax.shard_map(
        body,
        mesh=mesh,
        in_specs=(fields, fields, grid, grid, grid, P("shot"), P("shot"), P("shot", None), P("shot", None)),
        out_specs=(fields, fields, P(None, "tx", "ty", None)),
        check_vma=False,
    )
```

```python
import functools

import jax
import jax.numpy as jnp
from jax import lax
from jax.experimental import pallas as pl
from jax.experimental.pallas import tpu as pltpu
from jax.sharding import PartitionSpec as P

C1 = 9.0 / 8.0
C2 = -1.0 / 24.0
DT = 0.15
MESH = pl.DeviceIdType.MESH
F32 = jnp.float32
XX, YY, ZZ, XY, XZ, YZ = range(6)


def step_kernel(
    fwd, adj, lam_h, mu_h, den_h, source_h, rcell_h, ramp_h,
    f_out, a_out, g_out,
    ST, VE, VO, AC, BU, LM, MU, ADD, rcell, ramp, source,
    ysend, yrecv, rimsend, rimrecv, y2sb, y2sa, y2rb, y2ra,
    xs_send, xv_send, xe_send, xs_recv, xv_recv, xe_recv, rel_s, rel_v, GL, GR,
    in_sem, y_ss, y_rs, x_ss, x_rs, rel_ss, rel_rs, g_ss, g_rs,
):
    s, tx, ty = lax.axis_index("shot"), lax.axis_index("tx"), lax.axis_index("ty")
    last = lax.axis_size("ty") - 1
    partner = (1 - s, tx, ty)

    near_l, near_r = (tx > 0) & (tx != 4), (tx < 7) & (tx != 3)
    lower, upper = ty > 0, ty < last
    is3, is4 = tx == 3, tx == 4
    low_relay, high_relay = tx < 3, tx > 4

    bar = pltpu.get_barrier_semaphore()

    def greet(cond, dev):
        @pl.when(cond)
        def _():
            pl.semaphore_signal(bar, inc=1, device_id=dev, device_id_type=MESH)

    greet(is3, (s, 4, ty))
    greet(is4, (s, 3, ty))
    greet(lower, (s, tx, ty - 1))
    greet(upper, (s, tx, ty + 1))
    greet(near_l, (s, tx - 1, ty))
    greet(near_r, (s, tx + 1, ty))
    greet(tx < 2, (s, 3, ty))
    greet(tx > 5, (s, 4, ty))
    pl.semaphore_signal(bar, inc=1, device_id=partner, device_id_type=MESH)

    loads = [
        (fwd.at[0, pl.ds(3, 6)], ST.at[0, :, pl.ds(2, 16), pl.ds(8, 16)]),
        (adj.at[0, pl.ds(3, 6)], ST.at[1, :, pl.ds(2, 16), pl.ds(8, 16)]),
        (rcell_h, rcell),
        (ramp_h, ramp),
        (source_h, source),
        (den_h, BU.at[pl.ds(2, 16), pl.ds(8, 16)]),
        (fwd.at[0, pl.ds(0, 3)], VO.at[0]),
        (adj.at[0, pl.ds(0, 3)], VO.at[1]),
        (lam_h, LM),
        (mu_h, MU),
    ]
    copies = [pltpu.make_async_copy(a, b, in_sem.at[i]) for i, (a, b) in enumerate(loads)]
    for c in copies:
        c.start()

    def clear(cond, ref, idx):
        @pl.when(cond)
        def _():
            ref[idx] = jnp.zeros(ref.at[idx].shape, F32)

    for w in range(2):
        for c in (XX, XY, XZ):
            for lo in (0, 18):
                ST[w, c, lo:lo + 2, 8:24, :] = jnp.zeros((2, 16, 128), F32)
    for side, gone in ((0, ty == 0), (1, ty == last)):
        clear(gone, yrecv, side)
        clear(gone, rimrecv, side)
    clear(ty == 0, y2rb, slice(None))
    clear(ty == last, y2ra, slice(None))
    for side, gone in ((0, tx == 0), (1, tx == 7)):
        clear(gone, xs_recv, side)
        clear(gone, xv_recv, side)
        clear(gone, xe_recv, side)
    xe_send[...] = jnp.zeros(xe_send.shape, F32)
    for w in range(2):
        for c in (XY, YY, YZ):
            for lo in (0, 24):
                ST[w, c, 2:18, lo:lo + 8, :] = jnp.zeros((16, 8, 128), F32)
    rimsend[0, 0:4] = jnp.zeros((4, 8, 128), F32)

    for c in copies[2:5]:
        c.wait()

    def place(cell):
        lx = (cell >> 16) - tx * 16
        ly = ((cell >> 7) & 511) - ty * 16
        inside = (lx >= 0) & (lx < 16) & (ly >= 0) & (ly < 16)
        return jnp.where(inside, lx * 16 + ly, -1), cell & 127

    column, depth = place(rcell[...])
    hot = (lax.broadcasted_iota(jnp.int32, (256, 256), 0) == column).astype(jnp.bfloat16)
    amount = jnp.where(lax.broadcasted_iota(jnp.int32, (128, 256), 0) == depth, ramp[...], 0.0)
    high = amount.astype(jnp.bfloat16)
    rest = amount - high.astype(F32)
    mid = rest.astype(jnp.bfloat16)
    low = (rest - mid.astype(F32)).astype(jnp.bfloat16)
    nt = (((1,), (1,)), ((), ()))
    added = sum(
        lax.dot_general(hot, part, nt, preferred_element_type=F32) for part in (low, mid, high)
    )
    ADD[...] = added.reshape(16, 16, 128)
    copies[0].wait()
    copies[1].wait()

    def inject_rows(i, carry):
        shape = (2, 16, 128)
        gx = lax.broadcasted_iota(jnp.int32, shape, 0) + (2 * i + tx * 16)
        gy = lax.broadcasted_iota(jnp.int32, shape, 1) + ty * 16
        cell = gx * 65536 + gy * 128 + lax.broadcasted_iota(jnp.int32, shape, 2)
        src = jnp.where(cell.astype(F32) == source[0], source[1], 0.0)
        rows = pl.ds(2 + 2 * i, 2)
        for c in range(3):
            ST[0, c, rows, 8:24, :] = ST[0, c, rows, 8:24, :] + src
            ST[1, c, rows, 8:24, :] = ST[1, c, rows, 8:24, :] + ADD[pl.ds(2 * i, 2)]
        return carry

    lax.fori_loop(0, 8, inject_rows, 0)
    copies[5].wait()
    BU[2:18, 8:24, :] = DT / BU[2:18, 8:24, :]

    for w in range(2):
        layers = [(XX, 15), (XY, 14), (XY, 15), (XZ, 14), (XZ, 15)]
        for i, (c, x) in enumerate(layers):
            xs_send[0, 5 * w + i] = ST[w, c, 2 + x, 8:24, :]
        layers = [(XX, 0), (XX, 1), (XY, 0), (XZ, 0)]
        for i, (c, x) in enumerate(layers):
            xs_send[1, 4 * w + i] = ST[w, c, 2 + x, 8:24, :]
    for i in range(2):
        xv_send[0, 8 + i] = BU[16 + i, 8:24, :]
        xs_send[1, 8 + i] = BU[2 + i, 8:24, :]
    edges = (0, 1, 14, 15)
    for w in range(2):
        k = 4 * w
        for c, y, n in ((XY, 14, 2), (YZ, 14, 2)):
            ysend[0, 0:16, k:k + n, :] = ST[w, c, 2:18, 8 + y:8 + y + n, :]
            k += n
        for x in range(16):
            k = 16 * w + x
            ysend[0, 16 + k // 8, k % 8:k % 8 + 1, :] = ST[w, YY, 2 + x, 23:24, :]
        k = 4 * w
        for c, n in ((XY, 1), (YZ, 1), (YY, 2)):
            ysend[1, 0:16, k:k + n, :] = ST[w, c, 2:18, 8:8 + n, :]
            k += n
        for i, x in enumerate(edges):
            for q, c in enumerate((XX, XZ)):
                k = 2 * w + q
                rimsend[0, i, k:k + 1, :] = ST[w, c, 2 + x, 23:24, :]
                k = 4 * w + 2 * q
                rimsend[1, i, k:k + 2, :] = ST[w, c, 2 + x, 8:10, :]
    for i, x in enumerate(edges):
        rimsend[0, 4 + i] = BU[2 + x, 16:24, :]
        rimsend[1, 4 + i] = BU[2 + x, 8:16, :]

    zi = lax.broadcasted_iota(jnp.int32, (1, 1, 128), 2)
    up1 = (zi < 127).astype(F32)
    up2 = (zi < 126).astype(F32)
    dn1 = (zi > 0).astype(F32)
    dn2 = (zi > 1).astype(F32)

    def dpz(f):
        return (
            (C1 * up1) * pltpu.roll(f, 127, 2) - C1 * f
            + (C2 * up2) * pltpu.roll(f, 126, 2) - (C2 * dn1) * pltpu.roll(f, 1, 2)
        )

    def dmz(f):
        return (
            C1 * f - (C1 * dn1) * pltpu.roll(f, 1, 2)
            + (C2 * up1) * pltpu.roll(f, 127, 2) - (C2 * dn2) * pltpu.roll(f, 2, 2)
        )

    def getter(ref, w, x0, n):
        def get(c, dx=0, dy=0):
            return ref[w, c, pl.ds(2 + x0 + dx, n), 8 + dy:24 + dy, :]

        def dpx(c):
            return C1 * (get(c, 1) - get(c)) + C2 * (get(c, 2) - get(c, -1))

        def dmx(c):
            return C1 * (get(c) - get(c, -1)) + C2 * (get(c, 1) - get(c, -2))

        def dpy(c):
            return C1 * (get(c, 0, 1) - get(c)) + C2 * (get(c, 0, 2) - get(c, 0, -1))

        def dmy(c):
            return C1 * (get(c) - get(c, 0, -1)) + C2 * (get(c, 0, 1) - get(c, 0, -2))

        return get, dpx, dmx, dpy, dmy

    def accelerate(x0, n):
        scale = BU[pl.ds(2 + x0, n), 8:24, :]
        for w in range(2):
            get, dpx, dmx, dpy, dmy = getter(ST, w, x0, n)
            sums = (
                dpx(XX) + dmy(XY) + dmz(get(XZ)),
                dmx(XY) + dpy(YY) + dmz(get(YZ)),
                dmx(XZ) + dmy(YZ) + dpz(get(ZZ)),
            )
            for c in range(3):
                step = scale * sums[c]
                if w == 0:
                    AC[c, pl.ds(x0, n)] = step
                VE[w, c, pl.ds(2 + x0, n), 8:24, :] = VO[w, c, pl.ds(x0, n)] + step

    for c in copies[6:]:
        c.wait()
    accelerate(0, 2)
    accelerate(14, 2)

    for w in range(2):
        for i, (c, x) in enumerate([(0, 14), (0, 15), (1, 15), (2, 15)]):
            xv_send[0, 4 * w + i] = VE[w, c, 2 + x, 8:24, :]
        for i, (c, x) in enumerate([(0, 0), (1, 0), (1, 1), (2, 0), (2, 1)]):
            xv_send[1, 5 * w + i] = VE[w, c, 2 + x, 8:24, :]

    def one(cond):
        return jnp.where(cond, 1, 0)

    far_end = is3 | is4
    peers = 1 + one(lower) + one(upper) + one(near_l) + one(near_r) + 3 * one(far_end)
    pl.semaphore_wait(bar, peers)

    def remote(src, dst, ss, rs, dev):
        return pltpu.make_async_remote_copy(
            src_ref=src, dst_ref=dst, send_sem=ss, recv_sem=rs, device_id=dev, device_id_type=MESH
        )

    x_send = (xs_send, xv_send, xe_send)
    x_recv = (xs_recv, xv_recv, xe_recv)
    relay_buf = (rel_s, rel_v)

    def layers_of(kind, j):
        if j is None:
            return (pl.ds(0, 4), pl.ds(9, 1))[kind]
        return (pl.ds(4 + 2 * j, 2), pl.ds(3 * j, 3))[kind]

    def x_near(side, kind):
        dev = (s, tx + 1 if side == 0 else tx - 1, ty)
        return remote(
            x_send[kind].at[side], x_recv[kind].at[side], x_ss.at[side, kind, 0], x_rs.at[side, kind, 0], dev
        )

    def x_straight(side, kind):
        dev = (s, 4 if side == 0 else 3, ty)
        part = layers_of(kind, None)
        return remote(
            x_send[kind].at[side, part], x_recv[kind].at[side, part],
            x_ss.at[side, kind, 0], x_rs.at[side, kind, 0], dev,
        )

    def to_relay(side, kind, j):
        dev = (s, j if side == 0 else 5 + j, ty)
        return remote(
            x_send[kind].at[side, layers_of(kind, j)], relay_buf[kind],
            x_ss.at[side, kind, 1 + j], rel_rs.at[kind], dev,
        )

    def relay_on(side, kind, j):
        dev = (s, 4 if side == 0 else 3, ty)
        return remote(
            relay_buf[kind], x_recv[kind].at[side, layers_of(kind, j)],
            rel_ss.at[kind], x_rs.at[side, kind, 1 + j], dev,
        )

    near = (near_r, near_l)
    far = (is3, is4)
    near_recv = (near_l, near_r)
    far_recv = (is4, is3)

    def far_copies(side, kind):
        if kind == 2:
            return [x_near(side, 2)]
        return [to_relay(side, kind, j) for j in range(3)] + [x_straight(side, kind)]

    def send_x(kind):
        for side in range(2):
            @pl.when(far[side])
            def _():
                for cp in far_copies(side, kind):
                    cp.start()

            @pl.when(near[side])
            def _():
                x_near(side, kind).start()

    exists_send_y = (upper, lower)
    exists_recv_y = (lower, upper)

    def y_copy(side):
        dev = (s, tx, ty + 1 if side == 0 else ty - 1)
        part = pl.ds(0, 20) if side == 0 else pl.ds(0, 16)
        return remote(ysend.at[side, part], yrecv.at[side, part], y_ss.at[side, 0], y_rs.at[side, 0], dev)

    def rim_copy(side):
        dev = (s, tx, ty + 1 if side == 0 else ty - 1)
        return remote(rimsend.at[side], rimrecv.at[side], y_ss.at[side, 1], y_rs.at[side, 1], dev)

    def y2_copy(side):
        dev = (s, tx, ty + 1 if side == 0 else ty - 1)
        src, dst = ((y2sb, y2rb), (y2sa, y2ra))[side]
        return remote(src, dst, y_ss.at[side, 3], y_rs.at[side, 3], dev)

    for side in range(2):
        @pl.when(exists_send_y[side])
        def _():
            y_copy(side).start()
    send_x(0)
    send_x(1)
    for side in range(2):
        @pl.when(exists_send_y[side])
        def _():
            rim_copy(side).start()


    for side in range(2):
        @pl.when(exists_recv_y[side])
        def _():
            y_copy(side).wait_recv()

    for w in range(2):
        k = 4 * w
        ST[w, XY, 2:18, 6:8, :] = yrecv[0, 0:16, k:k + 2, :]
        ST[w, YZ, 2:18, 6:8, :] = yrecv[0, 0:16, k + 2:k + 4, :]
        ST[w, XY, 2:18, 24:25, :] = yrecv[1, 0:16, k:k + 1, :]
        ST[w, YZ, 2:18, 24:25, :] = yrecv[1, 0:16, k + 1:k + 2, :]
        ST[w, YY, 2:18, 24:26, :] = yrecv[1, 0:16, k + 2:k + 4, :]
        for x in range(16):
            k = 16 * w + x
            ST[w, YY, 2 + x, 7:8, :] = yrecv[0, 16 + k // 8, k % 8:k % 8 + 1, :]

    def accel_rows(i, carry):
        accelerate(2 * i, 2)
        return carry

    lax.fori_loop(0, 8, accel_rows, 0)

    for w in range(2):
        k = 4 * w
        for c, y, n in ((0, 15, 1), (1, 14, 2), (2, 15, 1)):
            y2sb[:, k:k + n, :] = VE[w, c, 2:18, 8 + y:8 + y + n, :]
            k += n
        k = 4 * w
        for c, n in ((0, 2), (1, 1), (2, 1)):
            y2sa[0:16, k:k + n, :] = VE[w, c, 2:18, 8:8 + n, :]
            k += n
        for x in range(16):
            k = 16 * w + x
            y2sa[16 + k // 8, k % 8:k % 8 + 1, :] = VE[w, 2, 2 + x, 9:10, :]
    for side in range(2):
        @pl.when(exists_send_y[side])
        def _():
            y2_copy(side).start()
    for side in range(2):
        @pl.when(exists_recv_y[side])
        def _():
            rim_copy(side).wait_recv()

    items = (
        [(XX, 15), (XY, 14), (XY, 15), (XZ, 14), (XZ, 15), (YY, 15), (YZ, 15)],
        [(XX, 0), (XX, 1), (XY, 0), (XZ, 0), (YY, 0), (YY, 1), (YZ, 0), (YZ, 1)],
    )
    for side in range(2):
        for w in range(2):
            for i, (c, x) in enumerate(items[side]):
                nb = 2 if c in (XY, YZ) else 1
                if c in (XX, XZ):
                    q, at = (0 if c == XX else 1), edges.index(x)
                    before = rimrecv[0, at, 2 * w + q:2 * w + q + 1, :]
                    after = rimrecv[1, at, 4 * w + 2 * q:4 * w + 2 * q + 2, :]
                else:
                    before = ST[w, c, 2 + x, 8 - nb:8, :]
                    after = ST[w, c, 2 + x, 24:27 - nb, :]
                xe_send[side, w, 3 * i:3 * i + nb, :] = before
                xe_send[side, w, 3 * i + nb:3 * i + 3, :] = after
    send_x(2)

    relays = (low_relay, high_relay)
    for side in range(2):
        @pl.when(relays[side])
        def _():
            j = tx if side == 0 else tx - 5
            for kind in range(2):
                to_relay(side, kind, 0).wait_recv()
                relay_on(side, kind, j).start()

    for side in range(2):
        @pl.when(exists_recv_y[side])
        def _():
            y2_copy(side).wait_recv()
    for w in range(2):
        k = 4 * w
        for c, n in ((0, 1), (1, 2), (2, 1)):
            VE[w, c, 2:18, 8 - n:8, :] = y2rb[:, k:k + n, :]
            k += n
        k = 4 * w
        for c, n in ((0, 2), (1, 1), (2, 1)):
            VE[w, c, 2:18, 24:24 + n, :] = y2ra[0:16, k:k + n, :]
            k += n
        for x in range(16):
            k = 16 * w + x
            VE[w, 2, 2 + x, 25:26, :] = y2ra[16 + k // 8, k % 8:k % 8 + 1, :]

    def finish(x0, n):
        lam = DT * LM[pl.ds(x0, n)]
        mu = DT * MU[pl.ds(x0, n)]
        rows = pl.ds(x0, n)
        kept = None
        for w, out in ((0, f_out), (1, a_out)):
            get, dpx, dmx, dpy, dmy = getter(VE, w, x0, n)
            vx, vy, vz = get(0), get(1), get(2)
            e = [
                dmx(0), dmy(1), dmz(vz),
                dpy(0) + dpx(1), dpz(vx) + dpx(2), dpz(vy) + dpy(2),
            ]
            trace = e[0] + e[1] + e[2]
            lt = lam * trace
            new = []
            for c in range(6):
                old = ST[w, c, pl.ds(2 + x0, n), 8:24, :]
                new.append(old + (lt + (2.0 * mu) * e[c]) if c < 3 else old + mu * e[c])
                out[3 + c, rows] = new[c]
            for c, v in enumerate((vx, vy, vz)):
                out[c, rows] = v
            if w == 0:
                kept = (trace, e)
            else:
                trace0, e0 = kept
                GL[0, rows] = (-DT) * trace0 * (new[0] + new[1] + new[2])
                prod = e0[0] * new[0]
                for c in range(1, 6):
                    prod = prod + e0[c] * new[c]
                GL[1, rows] = (-DT) * prod
                GL[2, rows] = -(AC[0, rows] * vx + AC[1, rows] * vy + AC[2, rows] * vz)

    def g_copy(k):
        lo, n = ((4, 8), (0, 4), (12, 4))[k]
        return remote(
            GL.at[:, pl.ds(lo, n)], GR.at[:, pl.ds(lo, n)], g_ss.at[k], g_rs.at[k], partner
        )

    def finish_rows(i, carry):
        finish(2 * i, 2)
        return carry

    lax.fori_loop(2, 6, finish_rows, 0)
    g_copy(0).start()

    def correct(w, c, x, e, terms):
        nb = 2 if c == 1 else 1
        lower_part = sum(k * xe_recv[e, w, 3 * i:3 * i + nb, :] for i, k in terms)
        upper_part = sum(k * xe_recv[e, w, 3 * i + nb:3 * i + 3, :] for i, k in terms)
        r = x if e == 0 else x - 14
        VE[w, c, 2 + x, 8 - nb:8, :] = VE[w, c, 2 + x, 8 - nb:8, :] + rimrecv[0, 4 + 2 * e + r, 8 - nb:8, :] * lower_part
        na = 3 - nb
        VE[w, c, 2 + x, 24:24 + na, :] = VE[w, c, 2 + x, 24:24 + na, :] + rimrecv[1, 4 + 2 * e + r, 0:na, :] * upper_part

    def rim(w, c, x, e, scale, i, forward):
        def f(k):
            return xe_recv[e, w, 3 * i + k:3 * i + k + 1, :]

        if forward:
            adds = ((0, -C2 * f(0)), (14, C2 * f(1)), (15, C1 * f(1) + C2 * f(2)))
        else:
            adds = ((0, -C1 * f(1) - C2 * f(0)), (1, -C2 * f(1)), (15, C2 * f(2)))
        for y, v in adds:
            VE[w, c, x, 8 + y:9 + y, :] = VE[w, c, x, 8 + y:9 + y, :] + scale[y:y + 1, :] * v

    def edge(side):
        @pl.when(near_recv[side])
        def _():
            for kind in range(3):
                x_near(side, kind).wait_recv()

        @pl.when(far_recv[side])
        def _():
            for kind in range(2):
                for j in range(3):
                    relay_on(side, kind, j).wait_recv()
                x_straight(side, kind).wait_recv()
            x_near(side, 2).wait_recv()

        def mine(w, c, x):
            return ST[w, c, 2 + x, 8:24, :]

        if side == 0:
            b2, b1 = xv_recv[0, 8], xv_recv[0, 9]
            for w in range(2):
                k = 5 * w
                ST[w, XX, 1, 8:24, :] = xs_recv[0, k]
                ST[w, XY, 0:2, 8:24, :] = xs_recv[0, k + 1:k + 3]
                ST[w, XZ, 0:2, 8:24, :] = xs_recv[0, k + 3:k + 5]
                k = 4 * w
                VE[w, 0, 0, 8:24, :] = xv_recv[0, k] + b2 * (C2 * mine(w, XX, 0))
                VE[w, 0, 1, 8:24, :] = xv_recv[0, k + 1] + b1 * (C1 * mine(w, XX, 0) + C2 * mine(w, XX, 1))
                VE[w, 1, 1, 8:24, :] = xv_recv[0, k + 2] + b1 * (C2 * mine(w, XY, 0))
                VE[w, 2, 1, 8:24, :] = xv_recv[0, k + 3] + b1 * (C2 * mine(w, XZ, 0))
                rim(w, 0, 0, 0, xv_recv.at[0, 8], 1, False)
                rim(w, 0, 1, 0, xv_recv.at[0, 9], 2, False)
                rim(w, 1, 1, 0, xv_recv.at[0, 9], 5, True)
                rim(w, 2, 1, 0, xv_recv.at[0, 9], 6, False)
                correct(w, 0, 0, 0, ((0, -C2),))
                correct(w, 1, 0, 0, ((2, -C1), (1, -C2)))
                correct(w, 1, 1, 0, ((2, -C2),))
                correct(w, 2, 0, 0, ((4, -C1), (3, -C2)))
                correct(w, 2, 1, 0, ((4, -C2),))
            accelerate(0, 2)
            first = 0
        else:
            b1, b2 = xs_recv[1, 8], xs_recv[1, 9]
            for w in range(2):
                k = 4 * w
                ST[w, XX, 18:20, 8:24, :] = xs_recv[1, k:k + 2]
                ST[w, XY, 18, 8:24, :] = xs_recv[1, k + 2]
                ST[w, XZ, 18, 8:24, :] = xs_recv[1, k + 3]
                k = 5 * w
                VE[w, 0, 18, 8:24, :] = xv_recv[1, k] - b1 * (C2 * mine(w, XX, 15))
                for c, st, at in ((1, XY, k + 1), (2, XZ, k + 3)):
                    VE[w, c, 18, 8:24, :] = xv_recv[1, at] - b1 * (C1 * mine(w, st, 15) + C2 * mine(w, st, 14))
                    VE[w, c, 19, 8:24, :] = xv_recv[1, at + 1] - b2 * (C2 * mine(w, st, 15))
                rim(w, 0, 18, 1, xs_recv.at[1, 8], 2, False)
                rim(w, 1, 18, 1, xs_recv.at[1, 8], 4, True)
                rim(w, 1, 19, 1, xs_recv.at[1, 9], 5, True)
                rim(w, 2, 18, 1, xs_recv.at[1, 8], 6, False)
                rim(w, 2, 19, 1, xs_recv.at[1, 9], 7, False)
                correct(w, 0, 14, 1, ((0, C2),))
                correct(w, 0, 15, 1, ((0, C1), (1, C2)))
                correct(w, 1, 15, 1, ((2, C2),))
                correct(w, 2, 15, 1, ((3, C2),))
            accelerate(14, 2)
            first = 6

        lax.fori_loop(first, first + 2, finish_rows, 0)
        g_copy(1 + side).start()

    @pl.when(jnp.logical_not(is4))
    def _():
        edge(0)

    edge(1)

    @pl.when(is4)
    def _():
        edge(0)

    for k, (lo, n) in enumerate(((4, 8), (0, 4), (12, 4))):
        g_copy(k).wait_recv()
        for c in range(3):
            g_out[c, lo:lo + n] = GL[c, lo:lo + n] + GR[c, lo:lo + n]

    for k in range(3):
        g_copy(k).wait_send()
    for side in range(2):
        @pl.when(exists_send_y[side])
        def _():
            y_copy(side).wait_send()
            rim_copy(side).wait_send()
            y2_copy(side).wait_send()

        @pl.when(near[side])
        def _():
            for kind in range(3):
                x_near(side, kind).wait_send()

        @pl.when(far[side])
        def _():
            for kind in range(3):
                for cp in far_copies(side, kind):
                    cp.wait_send()

        @pl.when(relays[side])
        def _():
            for kind in range(2):
                relay_on(side, kind, 0).wait_send()


def store_kernel(f, a, g, f_out, a_out, g_out, sem):
    copies = [
        pltpu.make_async_copy(src, dst, sem.at[i])
        for i, (src, dst) in enumerate(((f, f_out), (a, a_out), (g, g_out)))
    ]
    for c in copies:
        c.start()
    for c in copies:
        c.wait()


def body(fwd, adj, lam, mu, den, scell, samp, rcell, ramp):
    fields, grads = (9, 16, 16, 128), (3, 16, 16, 128)
    hbm = pl.BlockSpec(memory_space=pltpu.HBM)
    vmem = pl.BlockSpec(memory_space=pltpu.VMEM)
    dma = pltpu.SemaphoreType.DMA

    source = jnp.concatenate([scell.astype(F32), samp])

    def buf(*shape, dtype=F32):
        return pltpu.VMEM(shape, dtype)

    f, a, g = pl.pallas_call(
        step_kernel,
        out_shape=(pltpu.VMEM(fields, F32), pltpu.VMEM(fields, F32), pltpu.VMEM(grads, F32)),
        in_specs=[hbm] * 8,
        out_specs=(vmem, vmem, vmem),
        scratch_shapes=[
            buf(2, 6, 20, 32, 128), buf(2, 3, 20, 32, 128), buf(2, 3, 16, 16, 128), buf(3, 16, 16, 128),
            buf(20, 32, 128), buf(16, 16, 128), buf(16, 16, 128), buf(16, 16, 128),
            buf(1, 256, dtype=jnp.int32), buf(1, 256),
            pltpu.SMEM((2,), F32),
            buf(2, 20, 8, 128), buf(2, 20, 8, 128), buf(2, 8, 8, 128), buf(2, 8, 8, 128),
            buf(16, 8, 128), buf(20, 8, 128), buf(16, 8, 128), buf(20, 8, 128),
            buf(2, 10, 16, 128), buf(2, 10, 16, 128), buf(2, 2, 24, 128),
            buf(2, 10, 16, 128), buf(2, 10, 16, 128), buf(2, 2, 24, 128),
            buf(2, 16, 128), buf(3, 16, 128), buf(3, 16, 16, 128), buf(3, 16, 16, 128),
            dma((10,)), dma((2, 4)), dma((2, 4)), dma((2, 3, 4)), dma((2, 3, 4)),
            dma((2,)), dma((2,)), dma((3,)), dma((3,)),
        ],
        compiler_params=pltpu.CompilerParams(
            collective_id=1, has_side_effects=True, vmem_limit_bytes=56 * 1024 * 1024
        ),
        name="step",
    )(fwd, adj, lam, mu, den, source, rcell, ramp)
    f, a, g = pl.pallas_call(
        store_kernel,
        out_shape=tuple(jax.ShapeDtypeStruct(shape, F32) for shape in (fields, fields, grads)),
        in_specs=[vmem] * 3,
        out_specs=(hbm,) * 3,
        scratch_shapes=[dma((3,))],
        compiler_params=pltpu.CompilerParams(vmem_limit_bytes=16 * 1024 * 1024),
        name="store",
    )(f, a, g)
    return f[None], a[None], g


def solution(mesh):
    fields = P("shot", None, "tx", "ty", None)
    grid = P("tx", "ty", None)
    return jax.shard_map(
        body,
        mesh=mesh,
        in_specs=(fields, fields, grid, grid, grid, P("shot"), P("shot"), P("shot", None), P("shot", None)),
        out_specs=(fields, fields, P(None, "tx", "ty", None)),
        check_vma=False,
    )
```

```python
import functools

import jax
import jax.numpy as jnp
from jax import lax
from jax.experimental import pallas as pl
from jax.experimental.pallas import tpu as pltpu
from jax.sharding import PartitionSpec as P

C1 = 9.0 / 8.0
C2 = -1.0 / 24.0
DT = 0.15
MESH = pl.DeviceIdType.MESH
F32 = jnp.float32
XX, YY, ZZ, XY, XZ, YZ = range(6)


def step_kernel(
    fwd, adj, lam_h, mu_h, den_h, scell_h, samp_h, rcell_h, ramp_h,
    f_out, a_out, g_out,
    ST, VE, VO, AC, BU, LM, MU, ADD, rcell, ramp, scell, samp,
    ysend, yrecv, rimsend, rimrecv, y2sb, y2sa, y2rb, y2ra,
    xs_send, xv_send, xe_send, xs_recv, xv_recv, xe_recv, rel_s, rel_v, GL, GR,
    in_sem, y_ss, y_rs, x_ss, x_rs, rel_ss, rel_rs, g_ss, g_rs,
):
    s, tx, ty = lax.axis_index("shot"), lax.axis_index("tx"), lax.axis_index("ty")
    last = lax.axis_size("ty") - 1
    partner = (1 - s, tx, ty)

    near_l, near_r = (tx > 0) & (tx != 4), (tx < 7) & (tx != 3)
    lower, upper = ty > 0, ty < last
    is3, is4 = tx == 3, tx == 4
    low_relay, high_relay = tx < 3, tx > 4

    bar = pltpu.get_barrier_semaphore()

    def greet(cond, dev):
        @pl.when(cond)
        def _():
            pl.semaphore_signal(bar, inc=1, device_id=dev, device_id_type=MESH)

    greet(is3, (s, 4, ty))
    greet(is4, (s, 3, ty))
    greet(lower, (s, tx, ty - 1))
    greet(upper, (s, tx, ty + 1))
    greet(near_l, (s, tx - 1, ty))
    greet(near_r, (s, tx + 1, ty))
    greet(tx < 2, (s, 3, ty))
    greet(tx > 5, (s, 4, ty))
    pl.semaphore_signal(bar, inc=1, device_id=partner, device_id_type=MESH)

    loads = [
        (fwd.at[0, pl.ds(3, 6)], ST.at[0, :, pl.ds(2, 16), pl.ds(8, 16)]),
        (adj.at[0, pl.ds(3, 6)], ST.at[1, :, pl.ds(2, 16), pl.ds(8, 16)]),
        (rcell_h, rcell),
        (ramp_h, ramp),
        (scell_h, scell),
        (samp_h, samp),
        (den_h, BU.at[pl.ds(2, 16), pl.ds(8, 16)]),
        (fwd.at[0, pl.ds(0, 3)], VO.at[0]),
        (adj.at[0, pl.ds(0, 3)], VO.at[1]),
        (lam_h, LM),
        (mu_h, MU),
    ]
    copies = [pltpu.make_async_copy(a, b, in_sem.at[i]) for i, (a, b) in enumerate(loads)]
    for c in copies:
        c.start()

    def clear(cond, ref, idx):
        @pl.when(cond)
        def _():
            ref[idx] = jnp.zeros(ref.at[idx].shape, F32)

    for w in range(2):
        for c in (XX, XY, XZ):
            for lo in (0, 18):
                ST[w, c, lo:lo + 2, 8:24, :] = jnp.zeros((2, 16, 128), F32)
    for side, gone in ((0, ty == 0), (1, ty == last)):
        clear(gone, yrecv, side)
        clear(gone, rimrecv, side)
    clear(ty == 0, y2rb, slice(None))
    clear(ty == last, y2ra, slice(None))
    for side, gone in ((0, tx == 0), (1, tx == 7)):
        clear(gone, xs_recv, side)
        clear(gone, xv_recv, side)
        clear(gone, xe_recv, side)
    xe_send[...] = jnp.zeros(xe_send.shape, F32)
    for w in range(2):
        for c in (XY, YY, YZ):
            for lo in (0, 24):
                ST[w, c, 2:18, lo:lo + 8, :] = jnp.zeros((16, 8, 128), F32)
    rimsend[0, 0:4] = jnp.zeros((4, 8, 128), F32)

    for c in copies[2:6]:
        c.wait()

    def place(cell):
        lx = (cell >> 16) - tx * 16
        ly = ((cell >> 7) & 511) - ty * 16
        inside = (lx >= 0) & (lx < 16) & (ly >= 0) & (ly < 16)
        return jnp.where(inside, lx * 16 + ly, -1), cell & 127

    column, depth = place(rcell[...])
    hot = (lax.broadcasted_iota(jnp.int32, (256, 256), 0) == column).astype(jnp.bfloat16)
    amount = jnp.where(lax.broadcasted_iota(jnp.int32, (128, 256), 0) == depth, ramp[...], 0.0)
    high = amount.astype(jnp.bfloat16)
    rest = amount - high.astype(F32)
    mid = rest.astype(jnp.bfloat16)
    low = (rest - mid.astype(F32)).astype(jnp.bfloat16)
    nt = (((1,), (1,)), ((), ()))
    added = sum(
        lax.dot_general(hot, part, nt, preferred_element_type=F32) for part in (low, mid, high)
    )
    ADD[...] = added.reshape(16, 16, 128)
    copies[0].wait()
    copies[1].wait()

    def inject_rows(i, carry):
        shape = (2, 16, 128)
        gx = lax.broadcasted_iota(jnp.int32, shape, 0) + (2 * i + tx * 16)
        gy = lax.broadcasted_iota(jnp.int32, shape, 1) + ty * 16
        cell = gx * 65536 + gy * 128 + lax.broadcasted_iota(jnp.int32, shape, 2)
        src = jnp.where(cell == scell[0], samp[0], 0.0)
        rows = pl.ds(2 + 2 * i, 2)
        for c in range(3):
            ST[0, c, rows, 8:24, :] = ST[0, c, rows, 8:24, :] + src
            ST[1, c, rows, 8:24, :] = ST[1, c, rows, 8:24, :] + ADD[pl.ds(2 * i, 2)]
        return carry

    lax.fori_loop(0, 8, inject_rows, 0)
    copies[6].wait()
    BU[2:18, 8:24, :] = DT / BU[2:18, 8:24, :]

    for w in range(2):
        layers = [(XX, 15), (XY, 14), (XY, 15), (XZ, 14), (XZ, 15)]
        for i, (c, x) in enumerate(layers):
            xs_send[0, 5 * w + i] = ST[w, c, 2 + x, 8:24, :]
        layers = [(XX, 0), (XX, 1), (XY, 0), (XZ, 0)]
        for i, (c, x) in enumerate(layers):
            xs_send[1, 4 * w + i] = ST[w, c, 2 + x, 8:24, :]
    for i in range(2):
        xv_send[0, 8 + i] = BU[16 + i, 8:24, :]
        xs_send[1, 8 + i] = BU[2 + i, 8:24, :]
    edges = (0, 1, 14, 15)
    for w in range(2):
        k = 4 * w
        for c, y, n in ((XY, 14, 2), (YZ, 14, 2)):
            ysend[0, 0:16, k:k + n, :] = ST[w, c, 2:18, 8 + y:8 + y + n, :]
            k += n
        for x in range(16):
            k = 16 * w + x
            ysend[0, 16 + k // 8, k % 8:k % 8 + 1, :] = ST[w, YY, 2 + x, 23:24, :]
        k = 4 * w
        for c, n in ((XY, 1), (YZ, 1), (YY, 2)):
            ysend[1, 0:16, k:k + n, :] = ST[w, c, 2:18, 8:8 + n, :]
            k += n
        for i, x in enumerate(edges):
            for q, c in enumerate((XX, XZ)):
                k = 2 * w + q
                rimsend[0, i, k:k + 1, :] = ST[w, c, 2 + x, 23:24, :]
                k = 4 * w + 2 * q
                rimsend[1, i, k:k + 2, :] = ST[w, c, 2 + x, 8:10, :]
    for i, x in enumerate(edges):
        rimsend[0, 4 + i] = BU[2 + x, 16:24, :]
        rimsend[1, 4 + i] = BU[2 + x, 8:16, :]

    zi = lax.broadcasted_iota(jnp.int32, (1, 1, 128), 2)
    up1 = (zi < 127).astype(F32)
    up2 = (zi < 126).astype(F32)
    dn1 = (zi > 0).astype(F32)
    dn2 = (zi > 1).astype(F32)

    def dpz(f):
        return (
            (C1 * up1) * pltpu.roll(f, 127, 2) - C1 * f
            + (C2 * up2) * pltpu.roll(f, 126, 2) - (C2 * dn1) * pltpu.roll(f, 1, 2)
        )

    def dmz(f):
        return (
            C1 * f - (C1 * dn1) * pltpu.roll(f, 1, 2)
            + (C2 * up1) * pltpu.roll(f, 127, 2) - (C2 * dn2) * pltpu.roll(f, 2, 2)
        )

    def getter(ref, w, x0, n):
        def get(c, dx=0, dy=0):
            return ref[w, c, pl.ds(2 + x0 + dx, n), 8 + dy:24 + dy, :]

        def dpx(c):
            return C1 * (get(c, 1) - get(c)) + C2 * (get(c, 2) - get(c, -1))

        def dmx(c):
            return C1 * (get(c) - get(c, -1)) + C2 * (get(c, 1) - get(c, -2))

        def dpy(c):
            return C1 * (get(c, 0, 1) - get(c)) + C2 * (get(c, 0, 2) - get(c, 0, -1))

        def dmy(c):
            return C1 * (get(c) - get(c, 0, -1)) + C2 * (get(c, 0, 1) - get(c, 0, -2))

        return get, dpx, dmx, dpy, dmy

    def accelerate(x0, n):
        scale = BU[pl.ds(2 + x0, n), 8:24, :]
        for w in range(2):
            get, dpx, dmx, dpy, dmy = getter(ST, w, x0, n)
            sums = (
                dpx(XX) + dmy(XY) + dmz(get(XZ)),
                dmx(XY) + dpy(YY) + dmz(get(YZ)),
                dmx(XZ) + dmy(YZ) + dpz(get(ZZ)),
            )
            for c in range(3):
                step = scale * sums[c]
                if w == 0:
                    AC[c, pl.ds(x0, n)] = step
                VE[w, c, pl.ds(2 + x0, n), 8:24, :] = VO[w, c, pl.ds(x0, n)] + step

    for c in copies[7:]:
        c.wait()
    accelerate(0, 2)
    accelerate(14, 2)

    for w in range(2):
        for i, (c, x) in enumerate([(0, 14), (0, 15), (1, 15), (2, 15)]):
            xv_send[0, 4 * w + i] = VE[w, c, 2 + x, 8:24, :]
        for i, (c, x) in enumerate([(0, 0), (1, 0), (1, 1), (2, 0), (2, 1)]):
            xv_send[1, 5 * w + i] = VE[w, c, 2 + x, 8:24, :]

    def one(cond):
        return jnp.where(cond, 1, 0)

    far_end = is3 | is4
    peers = 1 + one(lower) + one(upper) + one(near_l) + one(near_r) + 3 * one(far_end)
    pl.semaphore_wait(bar, peers)

    def remote(src, dst, ss, rs, dev):
        return pltpu.make_async_remote_copy(
            src_ref=src, dst_ref=dst, send_sem=ss, recv_sem=rs, device_id=dev, device_id_type=MESH
        )

    x_send = (xs_send, xv_send, xe_send)
    x_recv = (xs_recv, xv_recv, xe_recv)
    relay_buf = (rel_s, rel_v)

    def layers_of(kind, j):
        if j is None:
            return (pl.ds(0, 4), pl.ds(9, 1))[kind]
        return (pl.ds(4 + 2 * j, 2), pl.ds(3 * j, 3))[kind]

    def x_near(side, kind):
        dev = (s, tx + 1 if side == 0 else tx - 1, ty)
        return remote(
            x_send[kind].at[side], x_recv[kind].at[side], x_ss.at[side, kind, 0], x_rs.at[side, kind, 0], dev
        )

    def x_straight(side, kind):
        dev = (s, 4 if side == 0 else 3, ty)
        part = layers_of(kind, None)
        return remote(
            x_send[kind].at[side, part], x_recv[kind].at[side, part],
            x_ss.at[side, kind, 0], x_rs.at[side, kind, 0], dev,
        )

    def to_relay(side, kind, j):
        dev = (s, j if side == 0 else 5 + j, ty)
        return remote(
            x_send[kind].at[side, layers_of(kind, j)], relay_buf[kind],
            x_ss.at[side, kind, 1 + j], rel_rs.at[kind], dev,
        )

    def relay_on(side, kind, j):
        dev = (s, 4 if side == 0 else 3, ty)
        return remote(
            relay_buf[kind], x_recv[kind].at[side, layers_of(kind, j)],
            rel_ss.at[kind], x_rs.at[side, kind, 1 + j], dev,
        )

    near = (near_r, near_l)
    far = (is3, is4)
    near_recv = (near_l, near_r)
    far_recv = (is4, is3)

    def far_copies(side, kind):
        if kind == 2:
            return [x_near(side, 2)]
        return [to_relay(side, kind, j) for j in range(3)] + [x_straight(side, kind)]

    def send_x(kind):
        for side in range(2):
            @pl.when(far[side])
            def _():
                for cp in far_copies(side, kind):
                    cp.start()

            @pl.when(near[side])
            def _():
                x_near(side, kind).start()

    exists_send_y = (upper, lower)
    exists_recv_y = (lower, upper)

    def y_copy(side):
        dev = (s, tx, ty + 1 if side == 0 else ty - 1)
        part = pl.ds(0, 20) if side == 0 else pl.ds(0, 16)
        return remote(ysend.at[side, part], yrecv.at[side, part], y_ss.at[side, 0], y_rs.at[side, 0], dev)

    def rim_copy(side):
        dev = (s, tx, ty + 1 if side == 0 else ty - 1)
        return remote(rimsend.at[side], rimrecv.at[side], y_ss.at[side, 1], y_rs.at[side, 1], dev)

    def y2_copy(side):
        dev = (s, tx, ty + 1 if side == 0 else ty - 1)
        src, dst = ((y2sb, y2rb), (y2sa, y2ra))[side]
        return remote(src, dst, y_ss.at[side, 3], y_rs.at[side, 3], dev)

    for side in range(2):
        @pl.when(exists_send_y[side])
        def _():
            y_copy(side).start()
    send_x(0)
    send_x(1)
    for side in range(2):
        @pl.when(exists_send_y[side])
        def _():
            rim_copy(side).start()


    for side in range(2):
        @pl.when(exists_recv_y[side])
        def _():
            y_copy(side).wait_recv()

    for w in range(2):
        k = 4 * w
        ST[w, XY, 2:18, 6:8, :] = yrecv[0, 0:16, k:k + 2, :]
        ST[w, YZ, 2:18, 6:8, :] = yrecv[0, 0:16, k + 2:k + 4, :]
        ST[w, XY, 2:18, 24:25, :] = yrecv[1, 0:16, k:k + 1, :]
        ST[w, YZ, 2:18, 24:25, :] = yrecv[1, 0:16, k + 1:k + 2, :]
        ST[w, YY, 2:18, 24:26, :] = yrecv[1, 0:16, k + 2:k + 4, :]
        for x in range(16):
            k = 16 * w + x
            ST[w, YY, 2 + x, 7:8, :] = yrecv[0, 16 + k // 8, k % 8:k % 8 + 1, :]

    def accel_rows(i, carry):
        accelerate(2 * i, 2)
        return carry

    lax.fori_loop(0, 8, accel_rows, 0)

    for w in range(2):
        k = 4 * w
        for c, y, n in ((0, 15, 1), (1, 14, 2), (2, 15, 1)):
            y2sb[:, k:k + n, :] = VE[w, c, 2:18, 8 + y:8 + y + n, :]
            k += n
        k = 4 * w
        for c, n in ((0, 2), (1, 1), (2, 1)):
            y2sa[0:16, k:k + n, :] = VE[w, c, 2:18, 8:8 + n, :]
            k += n
        for x in range(16):
            k = 16 * w + x
            y2sa[16 + k // 8, k % 8:k % 8 + 1, :] = VE[w, 2, 2 + x, 9:10, :]
    for side in range(2):
        @pl.when(exists_send_y[side])
        def _():
            y2_copy(side).start()
    for side in range(2):
        @pl.when(exists_recv_y[side])
        def _():
            rim_copy(side).wait_recv()

    items = (
        [(XX, 15), (XY, 14), (XY, 15), (XZ, 14), (XZ, 15), (YY, 15), (YZ, 15)],
        [(XX, 0), (XX, 1), (XY, 0), (XZ, 0), (YY, 0), (YY, 1), (YZ, 0), (YZ, 1)],
    )
    for side in range(2):
        for w in range(2):
            for i, (c, x) in enumerate(items[side]):
                nb = 2 if c in (XY, YZ) else 1
                if c in (XX, XZ):
                    q, at = (0 if c == XX else 1), edges.index(x)
                    before = rimrecv[0, at, 2 * w + q:2 * w + q + 1, :]
                    after = rimrecv[1, at, 4 * w + 2 * q:4 * w + 2 * q + 2, :]
                else:
                    before = ST[w, c, 2 + x, 8 - nb:8, :]
                    after = ST[w, c, 2 + x, 24:27 - nb, :]
                xe_send[side, w, 3 * i:3 * i + nb, :] = before
                xe_send[side, w, 3 * i + nb:3 * i + 3, :] = after
    send_x(2)

    relays = (low_relay, high_relay)
    for side in range(2):
        @pl.when(relays[side])
        def _():
            j = tx if side == 0 else tx - 5
            for kind in range(2):
                to_relay(side, kind, 0).wait_recv()
                relay_on(side, kind, j).start()

    for side in range(2):
        @pl.when(exists_recv_y[side])
        def _():
            y2_copy(side).wait_recv()
    for w in range(2):
        k = 4 * w
        for c, n in ((0, 1), (1, 2), (2, 1)):
            VE[w, c, 2:18, 8 - n:8, :] = y2rb[:, k:k + n, :]
            k += n
        k = 4 * w
        for c, n in ((0, 2), (1, 1), (2, 1)):
            VE[w, c, 2:18, 24:24 + n, :] = y2ra[0:16, k:k + n, :]
            k += n
        for x in range(16):
            k = 16 * w + x
            VE[w, 2, 2 + x, 25:26, :] = y2ra[16 + k // 8, k % 8:k % 8 + 1, :]

    def finish(x0, n):
        lam = DT * LM[pl.ds(x0, n)]
        mu = DT * MU[pl.ds(x0, n)]
        rows = pl.ds(x0, n)
        kept = None
        for w, out in ((0, f_out), (1, a_out)):
            get, dpx, dmx, dpy, dmy = getter(VE, w, x0, n)
            vx, vy, vz = get(0), get(1), get(2)
            e = [
                dmx(0), dmy(1), dmz(vz),
                dpy(0) + dpx(1), dpz(vx) + dpx(2), dpz(vy) + dpy(2),
            ]
            trace = e[0] + e[1] + e[2]
            lt = lam * trace
            new = []
            for c in range(6):
                old = ST[w, c, pl.ds(2 + x0, n), 8:24, :]
                new.append(old + (lt + (2.0 * mu) * e[c]) if c < 3 else old + mu * e[c])
                out[3 + c, rows] = new[c]
            for c, v in enumerate((vx, vy, vz)):
                out[c, rows] = v
            if w == 0:
                kept = (trace, e)
            else:
                trace0, e0 = kept
                GL[0, rows] = (-DT) * trace0 * (new[0] + new[1] + new[2])
                prod = e0[0] * new[0]
                for c in range(1, 6):
                    prod = prod + e0[c] * new[c]
                GL[1, rows] = (-DT) * prod
                GL[2, rows] = -(AC[0, rows] * vx + AC[1, rows] * vy + AC[2, rows] * vz)

    def g_copy(k):
        lo, n = ((4, 8), (0, 4), (12, 4))[k]
        return remote(
            GL.at[:, pl.ds(lo, n)], GR.at[:, pl.ds(lo, n)], g_ss.at[k], g_rs.at[k], partner
        )

    def finish_rows(i, carry):
        finish(2 * i, 2)
        return carry

    lax.fori_loop(2, 6, finish_rows, 0)
    g_copy(0).start()

    def correct(w, c, x, e, terms):
        nb = 2 if c == 1 else 1
        lower_part = sum(k * xe_recv[e, w, 3 * i:3 * i + nb, :] for i, k in terms)
        upper_part = sum(k * xe_recv[e, w, 3 * i + nb:3 * i + 3, :] for i, k in terms)
        r = x if e == 0 else x - 14
        VE[w, c, 2 + x, 8 - nb:8, :] = VE[w, c, 2 + x, 8 - nb:8, :] + rimrecv[0, 4 + 2 * e + r, 8 - nb:8, :] * lower_part
        na = 3 - nb
        VE[w, c, 2 + x, 24:24 + na, :] = VE[w, c, 2 + x, 24:24 + na, :] + rimrecv[1, 4 + 2 * e + r, 0:na, :] * upper_part

    def rim(w, c, x, e, scale, i, forward):
        def f(k):
            return xe_recv[e, w, 3 * i + k:3 * i + k + 1, :]

        if forward:
            adds = ((0, -C2 * f(0)), (14, C2 * f(1)), (15, C1 * f(1) + C2 * f(2)))
        else:
            adds = ((0, -C1 * f(1) - C2 * f(0)), (1, -C2 * f(1)), (15, C2 * f(2)))
        for y, v in adds:
            VE[w, c, x, 8 + y:9 + y, :] = VE[w, c, x, 8 + y:9 + y, :] + scale[y:y + 1, :] * v

    def edge(side):
        @pl.when(near_recv[side])
        def _():
            for kind in range(3):
                x_near(side, kind).wait_recv()

        @pl.when(far_recv[side])
        def _():
            for kind in range(2):
                for j in range(3):
                    relay_on(side, kind, j).wait_recv()
                x_straight(side, kind).wait_recv()
            x_near(side, 2).wait_recv()

        def mine(w, c, x):
            return ST[w, c, 2 + x, 8:24, :]

        if side == 0:
            b2, b1 = xv_recv[0, 8], xv_recv[0, 9]
            for w in range(2):
                k = 5 * w
                ST[w, XX, 1, 8:24, :] = xs_recv[0, k]
                ST[w, XY, 0:2, 8:24, :] = xs_recv[0, k + 1:k + 3]
                ST[w, XZ, 0:2, 8:24, :] = xs_recv[0, k + 3:k + 5]
                k = 4 * w
                VE[w, 0, 0, 8:24, :] = xv_recv[0, k] + b2 * (C2 * mine(w, XX, 0))
                VE[w, 0, 1, 8:24, :] = xv_recv[0, k + 1] + b1 * (C1 * mine(w, XX, 0) + C2 * mine(w, XX, 1))
                VE[w, 1, 1, 8:24, :] = xv_recv[0, k + 2] + b1 * (C2 * mine(w, XY, 0))
                VE[w, 2, 1, 8:24, :] = xv_recv[0, k + 3] + b1 * (C2 * mine(w, XZ, 0))
                rim(w, 0, 0, 0, xv_recv.at[0, 8], 1, False)
                rim(w, 0, 1, 0, xv_recv.at[0, 9], 2, False)
                rim(w, 1, 1, 0, xv_recv.at[0, 9], 5, True)
                rim(w, 2, 1, 0, xv_recv.at[0, 9], 6, False)
                correct(w, 0, 0, 0, ((0, -C2),))
                correct(w, 1, 0, 0, ((2, -C1), (1, -C2)))
                correct(w, 1, 1, 0, ((2, -C2),))
                correct(w, 2, 0, 0, ((4, -C1), (3, -C2)))
                correct(w, 2, 1, 0, ((4, -C2),))
            accelerate(0, 2)
            first = 0
        else:
            b1, b2 = xs_recv[1, 8], xs_recv[1, 9]
            for w in range(2):
                k = 4 * w
                ST[w, XX, 18:20, 8:24, :] = xs_recv[1, k:k + 2]
                ST[w, XY, 18, 8:24, :] = xs_recv[1, k + 2]
                ST[w, XZ, 18, 8:24, :] = xs_recv[1, k + 3]
                k = 5 * w
                VE[w, 0, 18, 8:24, :] = xv_recv[1, k] - b1 * (C2 * mine(w, XX, 15))
                for c, st, at in ((1, XY, k + 1), (2, XZ, k + 3)):
                    VE[w, c, 18, 8:24, :] = xv_recv[1, at] - b1 * (C1 * mine(w, st, 15) + C2 * mine(w, st, 14))
                    VE[w, c, 19, 8:24, :] = xv_recv[1, at + 1] - b2 * (C2 * mine(w, st, 15))
                rim(w, 0, 18, 1, xs_recv.at[1, 8], 2, False)
                rim(w, 1, 18, 1, xs_recv.at[1, 8], 4, True)
                rim(w, 1, 19, 1, xs_recv.at[1, 9], 5, True)
                rim(w, 2, 18, 1, xs_recv.at[1, 8], 6, False)
                rim(w, 2, 19, 1, xs_recv.at[1, 9], 7, False)
                correct(w, 0, 14, 1, ((0, C2),))
                correct(w, 0, 15, 1, ((0, C1), (1, C2)))
                correct(w, 1, 15, 1, ((2, C2),))
                correct(w, 2, 15, 1, ((3, C2),))
            accelerate(14, 2)
            first = 6

        lax.fori_loop(first, first + 2, finish_rows, 0)
        g_copy(1 + side).start()

    @pl.when(jnp.logical_not(is4))
    def _():
        edge(0)

    edge(1)

    @pl.when(is4)
    def _():
        edge(0)

    for k, (lo, n) in enumerate(((4, 8), (0, 4), (12, 4))):
        g_copy(k).wait_recv()
        for c in range(3):
            g_out[c, lo:lo + n] = GL[c, lo:lo + n] + GR[c, lo:lo + n]

    for k in range(3):
        g_copy(k).wait_send()
    for side in range(2):
        @pl.when(exists_send_y[side])
        def _():
            y_copy(side).wait_send()
            rim_copy(side).wait_send()
            y2_copy(side).wait_send()

        @pl.when(near[side])
        def _():
            for kind in range(3):
                x_near(side, kind).wait_send()

        @pl.when(far[side])
        def _():
            for kind in range(3):
                for cp in far_copies(side, kind):
                    cp.wait_send()

        @pl.when(relays[side])
        def _():
            for kind in range(2):
                relay_on(side, kind, 0).wait_send()


def store_kernel(f, a, g, f_out, a_out, g_out, sem):
    copies = [
        pltpu.make_async_copy(src, dst, sem.at[i])
        for i, (src, dst) in enumerate(((f, f_out), (a, a_out), (g, g_out)))
    ]
    for c in copies:
        c.start()
    for c in copies:
        c.wait()


def body(fwd, adj, lam, mu, den, scell, samp, rcell, ramp):
    fields, grads = (9, 16, 16, 128), (3, 16, 16, 128)
    hbm = pl.BlockSpec(memory_space=pltpu.HBM)
    vmem = pl.BlockSpec(memory_space=pltpu.VMEM)
    dma = pltpu.SemaphoreType.DMA

    def buf(*shape, dtype=F32):
        return pltpu.VMEM(shape, dtype)

    f, a, g = pl.pallas_call(
        step_kernel,
        out_shape=(pltpu.VMEM(fields, F32), pltpu.VMEM(fields, F32), pltpu.VMEM(grads, F32)),
        in_specs=[hbm] * 9,
        out_specs=(vmem, vmem, vmem),
        scratch_shapes=[
            buf(2, 6, 20, 32, 128), buf(2, 3, 20, 32, 128), buf(2, 3, 16, 16, 128), buf(3, 16, 16, 128),
            buf(20, 32, 128), buf(16, 16, 128), buf(16, 16, 128), buf(16, 16, 128),
            buf(1, 256, dtype=jnp.int32), buf(1, 256),
            pltpu.SMEM((1,), jnp.int32), pltpu.SMEM((1,), F32),
            buf(2, 20, 8, 128), buf(2, 20, 8, 128), buf(2, 8, 8, 128), buf(2, 8, 8, 128),
            buf(16, 8, 128), buf(20, 8, 128), buf(16, 8, 128), buf(20, 8, 128),
            buf(2, 10, 16, 128), buf(2, 10, 16, 128), buf(2, 2, 24, 128),
            buf(2, 10, 16, 128), buf(2, 10, 16, 128), buf(2, 2, 24, 128),
            buf(2, 16, 128), buf(3, 16, 128), buf(3, 16, 16, 128), buf(3, 16, 16, 128),
            dma((11,)), dma((2, 4)), dma((2, 4)), dma((2, 3, 4)), dma((2, 3, 4)),
            dma((2,)), dma((2,)), dma((3,)), dma((3,)),
        ],
        compiler_params=pltpu.CompilerParams(
            collective_id=1, has_side_effects=True, vmem_limit_bytes=56 * 1024 * 1024
        ),
        name="step",
    )(fwd, adj, lam, mu, den, scell, samp, rcell, ramp)
    f, a, g = pl.pallas_call(
        store_kernel,
        out_shape=tuple(jax.ShapeDtypeStruct(shape, F32) for shape in (fields, fields, grads)),
        in_specs=[vmem] * 3,
        out_specs=(hbm,) * 3,
        scratch_shapes=[dma((3,))],
        compiler_params=pltpu.CompilerParams(vmem_limit_bytes=16 * 1024 * 1024),
        name="store",
    )(f, a, g)
    return f[None], a[None], g


def solution(mesh):
    fields = P("shot", None, "tx", "ty", None)
    grid = P("tx", "ty", None)
    return jax.shard_map(
        body,
        mesh=mesh,
        in_specs=(fields, fields, grid, grid, grid, P("shot"), P("shot"), P("shot", None), P("shot", None)),
        out_specs=(fields, fields, P(None, "tx", "ty", None)),
        check_vma=False,
    )
```

```python
import functools

import jax
import jax.numpy as jnp
from jax import lax
from jax.experimental import pallas as pl
from jax.experimental.pallas import tpu as pltpu
from jax.sharding import PartitionSpec as P

C1 = 9.0 / 8.0
C2 = -1.0 / 24.0
DT = 0.15
MESH = pl.DeviceIdType.MESH
F32 = jnp.float32
XX, YY, ZZ, XY, XZ, YZ = range(6)


def step_kernel(
    fwd, adj, lam_h, mu_h, den_h, scell_h, samp_h, rcell_h, ramp_h,
    f_out, a_out, g_out,
    ST, VE, VO, AC, BU, LM, MU, ADD, rcell, ramp, scell, samp,
    ysend, yrecv, rimsend, rimrecv, y2sb, y2sa, y2rb, y2ra,
    xs_send, xv_send, xe_send, xs_recv, xv_recv, xe_recv, rel_s, rel_v, GL, GR,
    in_sem, y_ss, y_rs, x_ss, x_rs, rel_ss, rel_rs, g_ss, g_rs,
):
    s, tx, ty = lax.axis_index("shot"), lax.axis_index("tx"), lax.axis_index("ty")
    last = lax.axis_size("ty") - 1
    partner = (1 - s, tx, ty)

    near_l, near_r = (tx > 0) & (tx != 4), (tx < 7) & (tx != 3)
    lower, upper = ty > 0, ty < last
    is3, is4 = tx == 3, tx == 4
    low_relay, high_relay = tx < 3, tx > 4

    bar = pltpu.get_barrier_semaphore()

    def greet(cond, dev):
        @pl.when(cond)
        def _():
            pl.semaphore_signal(bar, inc=1, device_id=dev, device_id_type=MESH)

    greet(is3, (s, 4, ty))
    greet(is4, (s, 3, ty))
    greet(lower, (s, tx, ty - 1))
    greet(upper, (s, tx, ty + 1))
    greet(near_l, (s, tx - 1, ty))
    greet(near_r, (s, tx + 1, ty))
    greet(tx < 2, (s, 3, ty))
    greet(tx > 5, (s, 4, ty))
    pl.semaphore_signal(bar, inc=1, device_id=partner, device_id_type=MESH)

    loads = [
        (fwd.at[0, pl.ds(3, 6)], ST.at[0, :, pl.ds(2, 16), pl.ds(8, 16)]),
        (adj.at[0, pl.ds(3, 6)], ST.at[1, :, pl.ds(2, 16), pl.ds(8, 16)]),
        (rcell_h, rcell),
        (ramp_h, ramp),
        (scell_h, scell),
        (samp_h, samp),
        (den_h, BU.at[pl.ds(2, 16), pl.ds(8, 16)]),
        (fwd.at[0, pl.ds(0, 3)], VO.at[0]),
        (adj.at[0, pl.ds(0, 3)], VO.at[1]),
        (lam_h, LM),
        (mu_h, MU),
    ]
    copies = [pltpu.make_async_copy(a, b, in_sem.at[i]) for i, (a, b) in enumerate(loads)]
    for c in copies:
        c.start()

    def clear(cond, ref, idx):
        @pl.when(cond)
        def _():
            ref[idx] = jnp.zeros(ref.at[idx].shape, F32)

    for w in range(2):
        for c in (XX, XY, XZ):
            for lo in (0, 18):
                ST[w, c, lo:lo + 2, 8:24, :] = jnp.zeros((2, 16, 128), F32)
    for side, gone in ((0, ty == 0), (1, ty == last)):
        clear(gone, yrecv, side)
        clear(gone, rimrecv, side)
    clear(ty == 0, y2rb, slice(None))
    clear(ty == last, y2ra, slice(None))
    for side, gone in ((0, tx == 0), (1, tx == 7)):
        clear(gone, xs_recv, side)
        clear(gone, xv_recv, side)
        clear(gone, xe_recv, side)
    xe_send[...] = jnp.zeros(xe_send.shape, F32)
    for w in range(2):
        for c in (XY, YY, YZ):
            for lo in (0, 24):
                ST[w, c, 2:18, lo:lo + 8, :] = jnp.zeros((16, 8, 128), F32)
    rimsend[0, 0:4] = jnp.zeros((4, 8, 128), F32)

    for c in copies[2:6]:
        c.wait()

    def place(cell):
        lx = (cell >> 16) - tx * 16
        ly = ((cell >> 7) & 511) - ty * 16
        inside = (lx >= 0) & (lx < 16) & (ly >= 0) & (ly < 16)
        return jnp.where(inside, lx * 16 + ly, -1), cell & 127

    column, depth = place(rcell[...])
    hot = (lax.broadcasted_iota(jnp.int32, (256, 256), 0) == column).astype(jnp.bfloat16)
    amount = jnp.where(lax.broadcasted_iota(jnp.int32, (128, 256), 0) == depth, ramp[...], 0.0)
    high = amount.astype(jnp.bfloat16)
    rest = amount - high.astype(F32)
    mid = rest.astype(jnp.bfloat16)
    low = (rest - mid.astype(F32)).astype(jnp.bfloat16)
    nt = (((1,), (1,)), ((), ()))
    added = sum(
        lax.dot_general(hot, part, nt, preferred_element_type=F32) for part in (low, mid, high)
    )
    ADD[...] = added.reshape(16, 16, 128)
    copies[0].wait()
    copies[1].wait()

    def inject_rows(i, carry):
        shape = (2, 16, 128)
        gx = lax.broadcasted_iota(jnp.int32, shape, 0) + (2 * i + tx * 16)
        gy = lax.broadcasted_iota(jnp.int32, shape, 1) + ty * 16
        cell = gx * 65536 + gy * 128 + lax.broadcasted_iota(jnp.int32, shape, 2)
        src = jnp.where(cell == scell[0], samp[0], 0.0)
        rows = pl.ds(2 + 2 * i, 2)
        for c in range(3):
            ST[0, c, rows, 8:24, :] = ST[0, c, rows, 8:24, :] + src
            ST[1, c, rows, 8:24, :] = ST[1, c, rows, 8:24, :] + ADD[pl.ds(2 * i, 2)]
        return carry

    lax.fori_loop(0, 8, inject_rows, 0)
    copies[6].wait()
    BU[2:18, 8:24, :] = DT / BU[2:18, 8:24, :]

    for w in range(2):
        layers = [(XX, 15), (XY, 14), (XY, 15), (XZ, 14), (XZ, 15)]
        for i, (c, x) in enumerate(layers):
            xs_send[0, 5 * w + i] = ST[w, c, 2 + x, 8:24, :]
        layers = [(XX, 0), (XX, 1), (XY, 0), (XZ, 0)]
        for i, (c, x) in enumerate(layers):
            xs_send[1, 4 * w + i] = ST[w, c, 2 + x, 8:24, :]
    for i in range(2):
        xv_send[0, 8 + i] = BU[16 + i, 8:24, :]
        xs_send[1, 8 + i] = BU[2 + i, 8:24, :]
    edges = (0, 1, 14, 15)
    for w in range(2):
        k = 4 * w
        for c, y, n in ((XY, 14, 2), (YZ, 14, 2)):
            ysend[0, 0:16, k:k + n, :] = ST[w, c, 2:18, 8 + y:8 + y + n, :]
            k += n
        for x in range(16):
            k = 16 * w + x
            ysend[0, 16 + k // 8, k % 8:k % 8 + 1, :] = ST[w, YY, 2 + x, 23:24, :]
        k = 4 * w
        for c, n in ((XY, 1), (YZ, 1), (YY, 2)):
            ysend[1, 0:16, k:k + n, :] = ST[w, c, 2:18, 8:8 + n, :]
            k += n
        for i, x in enumerate(edges):
            for q, c in enumerate((XX, XZ)):
                k = 2 * w + q
                rimsend[0, i, k:k + 1, :] = ST[w, c, 2 + x, 23:24, :]
                k = 4 * w + 2 * q
                rimsend[1, i, k:k + 2, :] = ST[w, c, 2 + x, 8:10, :]
    for i, x in enumerate(edges):
        rimsend[0, 4 + i] = BU[2 + x, 16:24, :]
        rimsend[1, 4 + i] = BU[2 + x, 8:16, :]

    zi = lax.broadcasted_iota(jnp.int32, (1, 1, 128), 2)
    up1 = (zi < 127).astype(F32)
    up2 = (zi < 126).astype(F32)
    dn1 = (zi > 0).astype(F32)
    dn2 = (zi > 1).astype(F32)

    def dpz(f):
        return (
            (C1 * up1) * pltpu.roll(f, 127, 2) - C1 * f
            + (C2 * up2) * pltpu.roll(f, 126, 2) - (C2 * dn1) * pltpu.roll(f, 1, 2)
        )

    def dmz(f):
        return (
            C1 * f - (C1 * dn1) * pltpu.roll(f, 1, 2)
            + (C2 * up1) * pltpu.roll(f, 127, 2) - (C2 * dn2) * pltpu.roll(f, 2, 2)
        )

    def getter(ref, w, x0, n):
        def get(c, dx=0, dy=0):
            return ref[w, c, pl.ds(2 + x0 + dx, n), 8 + dy:24 + dy, :]

        def dpx(c):
            return C1 * (get(c, 1) - get(c)) + C2 * (get(c, 2) - get(c, -1))

        def dmx(c):
            return C1 * (get(c) - get(c, -1)) + C2 * (get(c, 1) - get(c, -2))

        def dpy(c):
            return C1 * (get(c, 0, 1) - get(c)) + C2 * (get(c, 0, 2) - get(c, 0, -1))

        def dmy(c):
            return C1 * (get(c) - get(c, 0, -1)) + C2 * (get(c, 0, 1) - get(c, 0, -2))

        return get, dpx, dmx, dpy, dmy

    def accelerate(x0, n):
        scale = BU[pl.ds(2 + x0, n), 8:24, :]
        for w in range(2):
            get, dpx, dmx, dpy, dmy = getter(ST, w, x0, n)
            sums = (
                dpx(XX) + dmy(XY) + dmz(get(XZ)),
                dmx(XY) + dpy(YY) + dmz(get(YZ)),
                dmx(XZ) + dmy(YZ) + dpz(get(ZZ)),
            )
            for c in range(3):
                step = scale * sums[c]
                if w == 0:
                    AC[c, pl.ds(x0, n)] = step
                VE[w, c, pl.ds(2 + x0, n), 8:24, :] = VO[w, c, pl.ds(x0, n)] + step

    for c in copies[7:]:
        c.wait()
    accelerate(0, 2)
    accelerate(14, 2)

    for w in range(2):
        for i, (c, x) in enumerate([(0, 14), (0, 15), (1, 15), (2, 15)]):
            xv_send[0, 4 * w + i] = VE[w, c, 2 + x, 8:24, :]
        for i, (c, x) in enumerate([(0, 0), (1, 0), (1, 1), (2, 0), (2, 1)]):
            xv_send[1, 5 * w + i] = VE[w, c, 2 + x, 8:24, :]

    def one(cond):
        return jnp.where(cond, 1, 0)

    far_end = is3 | is4
    peers = 1 + one(lower) + one(upper) + one(near_l) + one(near_r) + 3 * one(far_end)
    pl.semaphore_wait(bar, peers)

    def remote(src, dst, ss, rs, dev):
        return pltpu.make_async_remote_copy(
            src_ref=src, dst_ref=dst, send_sem=ss, recv_sem=rs, device_id=dev, device_id_type=MESH
        )

    x_send = (xs_send, xv_send, xe_send)
    x_recv = (xs_recv, xv_recv, xe_recv)
    relay_buf = (rel_s, rel_v)

    def layers_of(kind, j):
        if j is None:
            return (pl.ds(0, 4), pl.ds(9, 1))[kind]
        return (pl.ds(4 + 2 * j, 2), pl.ds(3 * j, 3))[kind]

    def x_near(side, kind):
        dev = (s, tx + 1 if side == 0 else tx - 1, ty)
        return remote(
            x_send[kind].at[side], x_recv[kind].at[side], x_ss.at[side, kind, 0], x_rs.at[side, kind, 0], dev
        )

    def x_straight(side, kind):
        dev = (s, 4 if side == 0 else 3, ty)
        part = layers_of(kind, None)
        return remote(
            x_send[kind].at[side, part], x_recv[kind].at[side, part],
            x_ss.at[side, kind, 0], x_rs.at[side, kind, 0], dev,
        )

    def to_relay(side, kind, j):
        dev = (s, j if side == 0 else 5 + j, ty)
        return remote(
            x_send[kind].at[side, layers_of(kind, j)], relay_buf[kind],
            x_ss.at[side, kind, 1 + j], rel_rs.at[kind], dev,
        )

    def relay_on(side, kind, j):
        dev = (s, 4 if side == 0 else 3, ty)
        return remote(
            relay_buf[kind], x_recv[kind].at[side, layers_of(kind, j)],
            rel_ss.at[kind], x_rs.at[side, kind, 1 + j], dev,
        )

    near = (near_r, near_l)
    far = (is3, is4)
    near_recv = (near_l, near_r)
    far_recv = (is4, is3)

    def far_copies(side, kind):
        if kind == 2:
            return [x_near(side, 2)]
        return [to_relay(side, kind, j) for j in range(3)] + [x_straight(side, kind)]

    def send_x(kind):
        for side in range(2):
            @pl.when(far[side])
            def _():
                for cp in far_copies(side, kind):
                    cp.start()

            @pl.when(near[side])
            def _():
                x_near(side, kind).start()

    exists_send_y = (upper, lower)
    exists_recv_y = (lower, upper)

    def y_copy(side):
        dev = (s, tx, ty + 1 if side == 0 else ty - 1)
        part = pl.ds(0, 20) if side == 0 else pl.ds(0, 16)
        return remote(ysend.at[side, part], yrecv.at[side, part], y_ss.at[side, 0], y_rs.at[side, 0], dev)

    def rim_copy(side):
        dev = (s, tx, ty + 1 if side == 0 else ty - 1)
        return remote(rimsend.at[side], rimrecv.at[side], y_ss.at[side, 1], y_rs.at[side, 1], dev)

    def y2_copy(side):
        dev = (s, tx, ty + 1 if side == 0 else ty - 1)
        src, dst = ((y2sb, y2rb), (y2sa, y2ra))[side]
        return remote(src, dst, y_ss.at[side, 3], y_rs.at[side, 3], dev)

    for side in range(2):
        @pl.when(exists_send_y[side])
        def _():
            y_copy(side).start()
    send_x(0)
    send_x(1)
    for side in range(2):
        @pl.when(exists_send_y[side])
        def _():
            rim_copy(side).start()


    for side in range(2):
        @pl.when(exists_recv_y[side])
        def _():
            y_copy(side).wait_recv()

    for w in range(2):
        k = 4 * w
        ST[w, XY, 2:18, 6:8, :] = yrecv[0, 0:16, k:k + 2, :]
        ST[w, YZ, 2:18, 6:8, :] = yrecv[0, 0:16, k + 2:k + 4, :]
        ST[w, XY, 2:18, 24:25, :] = yrecv[1, 0:16, k:k + 1, :]
        ST[w, YZ, 2:18, 24:25, :] = yrecv[1, 0:16, k + 1:k + 2, :]
        ST[w, YY, 2:18, 24:26, :] = yrecv[1, 0:16, k + 2:k + 4, :]
        for x in range(16):
            k = 16 * w + x
            ST[w, YY, 2 + x, 7:8, :] = yrecv[0, 16 + k // 8, k % 8:k % 8 + 1, :]

    def accel_rows(i, carry):
        accelerate(2 * i, 2)
        return carry

    lax.fori_loop(0, 8, accel_rows, 0, unroll=True)

    for w in range(2):
        k = 4 * w
        for c, y, n in ((0, 15, 1), (1, 14, 2), (2, 15, 1)):
            y2sb[:, k:k + n, :] = VE[w, c, 2:18, 8 + y:8 + y + n, :]
            k += n
        k = 4 * w
        for c, n in ((0, 2), (1, 1), (2, 1)):
            y2sa[0:16, k:k + n, :] = VE[w, c, 2:18, 8:8 + n, :]
            k += n
        for x in range(16):
            k = 16 * w + x
            y2sa[16 + k // 8, k % 8:k % 8 + 1, :] = VE[w, 2, 2 + x, 9:10, :]
    for side in range(2):
        @pl.when(exists_send_y[side])
        def _():
            y2_copy(side).start()
    for side in range(2):
        @pl.when(exists_recv_y[side])
        def _():
            rim_copy(side).wait_recv()

    items = (
        [(XX, 15), (XY, 14), (XY, 15), (XZ, 14), (XZ, 15), (YY, 15), (YZ, 15)],
        [(XX, 0), (XX, 1), (XY, 0), (XZ, 0), (YY, 0), (YY, 1), (YZ, 0), (YZ, 1)],
    )
    for side in range(2):
        for w in range(2):
            for i, (c, x) in enumerate(items[side]):
                nb = 2 if c in (XY, YZ) else 1
                if c in (XX, XZ):
                    q, at = (0 if c == XX else 1), edges.index(x)
                    before = rimrecv[0, at, 2 * w + q:2 * w + q + 1, :]
                    after = rimrecv[1, at, 4 * w + 2 * q:4 * w + 2 * q + 2, :]
                else:
                    before = ST[w, c, 2 + x, 8 - nb:8, :]
                    after = ST[w, c, 2 + x, 24:27 - nb, :]
                xe_send[side, w, 3 * i:3 * i + nb, :] = before
                xe_send[side, w, 3 * i + nb:3 * i + 3, :] = after
    send_x(2)

    relays = (low_relay, high_relay)
    for side in range(2):
        @pl.when(relays[side])
        def _():
            j = tx if side == 0 else tx - 5
            for kind in range(2):
                to_relay(side, kind, 0).wait_recv()
                relay_on(side, kind, j).start()

    for side in range(2):
        @pl.when(exists_recv_y[side])
        def _():
            y2_copy(side).wait_recv()
    for w in range(2):
        k = 4 * w
        for c, n in ((0, 1), (1, 2), (2, 1)):
            VE[w, c, 2:18, 8 - n:8, :] = y2rb[:, k:k + n, :]
            k += n
        k = 4 * w
        for c, n in ((0, 2), (1, 1), (2, 1)):
            VE[w, c, 2:18, 24:24 + n, :] = y2ra[0:16, k:k + n, :]
            k += n
        for x in range(16):
            k = 16 * w + x
            VE[w, 2, 2 + x, 25:26, :] = y2ra[16 + k // 8, k % 8:k % 8 + 1, :]

    def finish(x0, n):
        lam = DT * LM[pl.ds(x0, n)]
        mu = DT * MU[pl.ds(x0, n)]
        rows = pl.ds(x0, n)
        kept = None
        for w, out in ((0, f_out), (1, a_out)):
            get, dpx, dmx, dpy, dmy = getter(VE, w, x0, n)
            vx, vy, vz = get(0), get(1), get(2)
            e = [
                dmx(0), dmy(1), dmz(vz),
                dpy(0) + dpx(1), dpz(vx) + dpx(2), dpz(vy) + dpy(2),
            ]
            trace = e[0] + e[1] + e[2]
            lt = lam * trace
            new = []
            for c in range(6):
                old = ST[w, c, pl.ds(2 + x0, n), 8:24, :]
                new.append(old + (lt + (2.0 * mu) * e[c]) if c < 3 else old + mu * e[c])
                out[3 + c, rows] = new[c]
            for c, v in enumerate((vx, vy, vz)):
                out[c, rows] = v
            if w == 0:
                kept = (trace, e)
            else:
                trace0, e0 = kept
                GL[0, rows] = (-DT) * trace0 * (new[0] + new[1] + new[2])
                prod = e0[0] * new[0]
                for c in range(1, 6):
                    prod = prod + e0[c] * new[c]
                GL[1, rows] = (-DT) * prod
                GL[2, rows] = -(AC[0, rows] * vx + AC[1, rows] * vy + AC[2, rows] * vz)

    def g_copy(k):
        lo, n = ((4, 8), (0, 4), (12, 4))[k]
        return remote(
            GL.at[:, pl.ds(lo, n)], GR.at[:, pl.ds(lo, n)], g_ss.at[k], g_rs.at[k], partner
        )

    def finish_rows(i, carry):
        finish(2 * i, 2)
        return carry

    lax.fori_loop(2, 6, finish_rows, 0, unroll=True)
    g_copy(0).start()

    def correct(w, c, x, e, terms):
        nb = 2 if c == 1 else 1
        lower_part = sum(k * xe_recv[e, w, 3 * i:3 * i + nb, :] for i, k in terms)
        upper_part = sum(k * xe_recv[e, w, 3 * i + nb:3 * i + 3, :] for i, k in terms)
        r = x if e == 0 else x - 14
        VE[w, c, 2 + x, 8 - nb:8, :] = VE[w, c, 2 + x, 8 - nb:8, :] + rimrecv[0, 4 + 2 * e + r, 8 - nb:8, :] * lower_part
        na = 3 - nb
        VE[w, c, 2 + x, 24:24 + na, :] = VE[w, c, 2 + x, 24:24 + na, :] + rimrecv[1, 4 + 2 * e + r, 0:na, :] * upper_part

    def rim(w, c, x, e, scale, i, forward):
        def f(k):
            return xe_recv[e, w, 3 * i + k:3 * i + k + 1, :]

        if forward:
            adds = ((0, -C2 * f(0)), (14, C2 * f(1)), (15, C1 * f(1) + C2 * f(2)))
        else:
            adds = ((0, -C1 * f(1) - C2 * f(0)), (1, -C2 * f(1)), (15, C2 * f(2)))
        for y, v in adds:
            VE[w, c, x, 8 + y:9 + y, :] = VE[w, c, x, 8 + y:9 + y, :] + scale[y:y + 1, :] * v

    def edge(side):
        @pl.when(near_recv[side])
        def _():
            for kind in range(3):
                x_near(side, kind).wait_recv()

        @pl.when(far_recv[side])
        def _():
            for kind in range(2):
                for j in range(3):
                    relay_on(side, kind, j).wait_recv()
                x_straight(side, kind).wait_recv()
            x_near(side, 2).wait_recv()

        def mine(w, c, x):
            return ST[w, c, 2 + x, 8:24, :]

        if side == 0:
            b2, b1 = xv_recv[0, 8], xv_recv[0, 9]
            for w in range(2):
                k = 5 * w
                ST[w, XX, 1, 8:24, :] = xs_recv[0, k]
                ST[w, XY, 0:2, 8:24, :] = xs_recv[0, k + 1:k + 3]
                ST[w, XZ, 0:2, 8:24, :] = xs_recv[0, k + 3:k + 5]
                k = 4 * w
                VE[w, 0, 0, 8:24, :] = xv_recv[0, k] + b2 * (C2 * mine(w, XX, 0))
                VE[w, 0, 1, 8:24, :] = xv_recv[0, k + 1] + b1 * (C1 * mine(w, XX, 0) + C2 * mine(w, XX, 1))
                VE[w, 1, 1, 8:24, :] = xv_recv[0, k + 2] + b1 * (C2 * mine(w, XY, 0))
                VE[w, 2, 1, 8:24, :] = xv_recv[0, k + 3] + b1 * (C2 * mine(w, XZ, 0))
                rim(w, 0, 0, 0, xv_recv.at[0, 8], 1, False)
                rim(w, 0, 1, 0, xv_recv.at[0, 9], 2, False)
                rim(w, 1, 1, 0, xv_recv.at[0, 9], 5, True)
                rim(w, 2, 1, 0, xv_recv.at[0, 9], 6, False)
                correct(w, 0, 0, 0, ((0, -C2),))
                correct(w, 1, 0, 0, ((2, -C1), (1, -C2)))
                correct(w, 1, 1, 0, ((2, -C2),))
                correct(w, 2, 0, 0, ((4, -C1), (3, -C2)))
                correct(w, 2, 1, 0, ((4, -C2),))
            accelerate(0, 2)
            first = 0
        else:
            b1, b2 = xs_recv[1, 8], xs_recv[1, 9]
            for w in range(2):
                k = 4 * w
                ST[w, XX, 18:20, 8:24, :] = xs_recv[1, k:k + 2]
                ST[w, XY, 18, 8:24, :] = xs_recv[1, k + 2]
                ST[w, XZ, 18, 8:24, :] = xs_recv[1, k + 3]
                k = 5 * w
                VE[w, 0, 18, 8:24, :] = xv_recv[1, k] - b1 * (C2 * mine(w, XX, 15))
                for c, st, at in ((1, XY, k + 1), (2, XZ, k + 3)):
                    VE[w, c, 18, 8:24, :] = xv_recv[1, at] - b1 * (C1 * mine(w, st, 15) + C2 * mine(w, st, 14))
                    VE[w, c, 19, 8:24, :] = xv_recv[1, at + 1] - b2 * (C2 * mine(w, st, 15))
                rim(w, 0, 18, 1, xs_recv.at[1, 8], 2, False)
                rim(w, 1, 18, 1, xs_recv.at[1, 8], 4, True)
                rim(w, 1, 19, 1, xs_recv.at[1, 9], 5, True)
                rim(w, 2, 18, 1, xs_recv.at[1, 8], 6, False)
                rim(w, 2, 19, 1, xs_recv.at[1, 9], 7, False)
                correct(w, 0, 14, 1, ((0, C2),))
                correct(w, 0, 15, 1, ((0, C1), (1, C2)))
                correct(w, 1, 15, 1, ((2, C2),))
                correct(w, 2, 15, 1, ((3, C2),))
            accelerate(14, 2)
            first = 6

        lax.fori_loop(first, first + 2, finish_rows, 0, unroll=True)
        g_copy(1 + side).start()

    @pl.when(jnp.logical_not(is4))
    def _():
        edge(0)

    edge(1)

    @pl.when(is4)
    def _():
        edge(0)

    for k, (lo, n) in enumerate(((4, 8), (0, 4), (12, 4))):
        g_copy(k).wait_recv()
        for c in range(3):
            g_out[c, lo:lo + n] = GL[c, lo:lo + n] + GR[c, lo:lo + n]

    for k in range(3):
        g_copy(k).wait_send()
    for side in range(2):
        @pl.when(exists_send_y[side])
        def _():
            y_copy(side).wait_send()
            rim_copy(side).wait_send()
            y2_copy(side).wait_send()

        @pl.when(near[side])
        def _():
            for kind in range(3):
                x_near(side, kind).wait_send()

        @pl.when(far[side])
        def _():
            for kind in range(3):
                for cp in far_copies(side, kind):
                    cp.wait_send()

        @pl.when(relays[side])
        def _():
            for kind in range(2):
                relay_on(side, kind, 0).wait_send()


def store_kernel(f, a, g, f_out, a_out, g_out, sem):
    copies = [
        pltpu.make_async_copy(src, dst, sem.at[i])
        for i, (src, dst) in enumerate(((f, f_out), (a, a_out), (g, g_out)))
    ]
    for c in copies:
        c.start()
    for c in copies:
        c.wait()


def body(fwd, adj, lam, mu, den, scell, samp, rcell, ramp):
    fields, grads = (9, 16, 16, 128), (3, 16, 16, 128)
    hbm = pl.BlockSpec(memory_space=pltpu.HBM)
    vmem = pl.BlockSpec(memory_space=pltpu.VMEM)
    dma = pltpu.SemaphoreType.DMA

    def buf(*shape, dtype=F32):
        return pltpu.VMEM(shape, dtype)

    f, a, g = pl.pallas_call(
        step_kernel,
        out_shape=(pltpu.VMEM(fields, F32), pltpu.VMEM(fields, F32), pltpu.VMEM(grads, F32)),
        in_specs=[hbm] * 9,
        out_specs=(vmem, vmem, vmem),
        scratch_shapes=[
            buf(2, 6, 20, 32, 128), buf(2, 3, 20, 32, 128), buf(2, 3, 16, 16, 128), buf(3, 16, 16, 128),
            buf(20, 32, 128), buf(16, 16, 128), buf(16, 16, 128), buf(16, 16, 128),
            buf(1, 256, dtype=jnp.int32), buf(1, 256),
            pltpu.SMEM((1,), jnp.int32), pltpu.SMEM((1,), F32),
            buf(2, 20, 8, 128), buf(2, 20, 8, 128), buf(2, 8, 8, 128), buf(2, 8, 8, 128),
            buf(16, 8, 128), buf(20, 8, 128), buf(16, 8, 128), buf(20, 8, 128),
            buf(2, 10, 16, 128), buf(2, 10, 16, 128), buf(2, 2, 24, 128),
            buf(2, 10, 16, 128), buf(2, 10, 16, 128), buf(2, 2, 24, 128),
            buf(2, 16, 128), buf(3, 16, 128), buf(3, 16, 16, 128), buf(3, 16, 16, 128),
            dma((11,)), dma((2, 4)), dma((2, 4)), dma((2, 3, 4)), dma((2, 3, 4)),
            dma((2,)), dma((2,)), dma((3,)), dma((3,)),
        ],
        compiler_params=pltpu.CompilerParams(
            collective_id=1, has_side_effects=True, vmem_limit_bytes=56 * 1024 * 1024
        ),
        name="step",
    )(fwd, adj, lam, mu, den, scell, samp, rcell, ramp)
    f, a, g = pl.pallas_call(
        store_kernel,
        out_shape=tuple(jax.ShapeDtypeStruct(shape, F32) for shape in (fields, fields, grads)),
        in_specs=[vmem] * 3,
        out_specs=(hbm,) * 3,
        scratch_shapes=[dma((3,))],
        compiler_params=pltpu.CompilerParams(vmem_limit_bytes=16 * 1024 * 1024),
        name="store",
    )(f, a, g)
    return f[None], a[None], g


def solution(mesh):
    fields = P("shot", None, "tx", "ty", None)
    grid = P("tx", "ty", None)
    return jax.shard_map(
        body,
        mesh=mesh,
        in_specs=(fields, fields, grid, grid, grid, P("shot"), P("shot"), P("shot", None), P("shot", None)),
        out_specs=(fields, fields, P(None, "tx", "ty", None)),
        check_vma=False,
    )
```
